256 devices in a mesh: cell: 64 (over y, z, core), spot: 4 (over x).
Axes of the slice: x: 4, y: 4, z: 8, core: 2. Of those that a mesh axis runs over, the one named last changes fastest.
Arguments:
- cells_pca: float32 [50, 32768], P(None, 'cell'), may hold values from -8 to 8
- spots_pca: float32 [50, 32768], P(None, ('spot', 'cell')), may hold values from -8 to 8
- log_a: float32 [32768], P('cell'), may hold values from -1 to 1
- log_b: float32 [32768], P('spot'), may hold values from -1 to 1
Outputs:
- cell_potential: float32 [32768], P('cell')
- spot_potential: float32 [32768], P('spot')
- barycenter: float32 [50, 32768], P(None, 'cell')
The draws below stay inside these ranges and needn't reach their ends.
All inputs are finite; a program needn't handle non-finite values.
Results may differ from the reference program's by a relative error of at most 0.0003.
Values sent between devices are 32-bit elements; how exact they have to be, the bound alone decides.
A program may use at most 128 MiB of HBM per device.

```python
import math
import jax
import jax.numpy as jnp
from jax import lax

PC = 50
ITERS = 2
NC = 32768
NS = 32768


def draw_points(key, comps, count):
    first = jax.random.fold_in(key, 0)
    return 0.15 * jnp.clip(jax.random.normal(first, (comps, count), jnp.float32), -6.0, 6.0)


def draw_cells_pca(key, part):
    key = jax.random.fold_in(key, 11)
    return draw_points(key, PC, NC)


def draw_spots_pca(key, part):
    key = jax.random.fold_in(key, 23)
    return draw_points(key, PC, NS)


def block_scale(key, extent, pieces, least, top_value):
    loudness, own = 1.0, jax.random.fold_in(key, 6)
    for position, blocks in pieces:
        steps = jnp.exp(jax.random.uniform(jax.random.fold_in(own, position), (blocks,), jnp.float32, least / len(pieces), top_value / len(pieces)))
        loudness = loudness * jnp.repeat(steps, extent[position] // blocks).reshape([-1 if axis == position else 1 for axis in range(len(extent))])
    return loudness


def setup_inputs(seed: int = 0) -> dict:
    splits = jax.random.split(jax.random.key(seed), 5)
    return {
        "cells_pca": draw_cells_pca(jax.random.fold_in(splits[4], 71), 0),
        "spots_pca": draw_spots_pca(jax.random.fold_in(splits[4], 71), 0),
        "log_a": jnp.clip(jax.random.uniform(splits[2], (NC,), jnp.float32, -1.0, 1.0) * block_scale(splits[2], (NC,), ((0, 64),), -0.4, 0.0), -1.0, 1.0),
        "log_b": jnp.clip(jax.random.uniform(splits[3], (NS,), jnp.float32, -1.0, 1.0) * block_scale(splits[3], (NS,), ((0, 4),), -0.4, 0.0), -1.0, 1.0),
    }


blur = 0.25


def cost_of(cell_block, cell_norm_block, spots, spot_norm):
    cross = jnp.dot(cell_block.T, spots, precision=lax.Precision.HIGHEST, preferred_element_type=jnp.float32)
    return (cell_norm_block[:, None] + spot_norm[None, :]) - 2.0 * cross


def reference(cells_pca, spots_pca, log_a, log_b):
    row_block = math.gcd(NC, 512)
    blocks = NC // row_block
    cell_norm = jnp.sum(cells_pca * cells_pca, axis=0)
    spot_norm = jnp.sum(spots_pca * spots_pca, axis=0)
    cell_blocks = cells_pca.reshape(PC, blocks, row_block).transpose(1, 0, 2)
    norm_blocks = cell_norm.reshape(blocks, row_block)
    mass_blocks = log_a.reshape(blocks, row_block)
    spot_potential = jnp.zeros((NS,), jnp.float32)
    cell_potential = jnp.zeros((NC,), jnp.float32)
    for step in range(ITERS):
        def row_pass(items):
            cell_block, norm_block, mass_block = items
            scores = (spot_potential[None, :] - cost_of(cell_block, norm_block, spots_pca, spot_norm)) / blur
            top = jnp.max(scores, axis=1)
            total = jnp.sum(jnp.exp(scores - top[:, None]), axis=1)
            return blur * mass_block - blur * (top + jnp.log(total))

        cell_potential = lax.map(row_pass, (cell_blocks, norm_blocks, mass_blocks)).reshape(NC)
        potential_blocks = cell_potential.reshape(blocks, row_block)

        def col_pass(carry, items):
            top, total = carry
            cell_block, norm_block, pot_block = items
            scores = (pot_block[:, None] - cost_of(cell_block, norm_block, spots_pca, spot_norm)) / blur
            new_top = jnp.maximum(top, jnp.max(scores, axis=0))
            total = total * jnp.exp(top - new_top) + jnp.sum(jnp.exp(scores - new_top[None, :]), axis=0)
            return (new_top, total), None

        start = (jnp.full((NS,), -jnp.inf, jnp.float32), jnp.zeros((NS,), jnp.float32))
        (top, total), unused = lax.scan(col_pass, start, (cell_blocks, norm_blocks, potential_blocks))
        spot_potential = blur * log_b - blur * (top + jnp.log(total))

    def bary_pass(items):
        cell_block, norm_block = items
        scores = (spot_potential[None, :] - cost_of(cell_block, norm_block, spots_pca, spot_norm)) / blur
        top = jnp.max(scores, axis=1)
        weight = jnp.exp(scores - top[:, None])
        numer = jnp.dot(spots_pca, weight.T, precision=lax.Precision.HIGHEST, preferred_element_type=jnp.float32)
        return numer / jnp.sum(weight, axis=1)[None, :]

    barycenter = lax.map(bary_pass, (cell_blocks, norm_blocks)).transpose(1, 0, 2).reshape(PC, NC)
    return cell_potential, spot_potential, barycenter
```

```python
import math

import jax
import jax.numpy as jnp
from jax import lax
from jax.experimental import pallas as pl
from jax.experimental.pallas import tpu as pltpu
from jax.sharding import PartitionSpec as P

MESH = pl.DeviceIdType.MESH
F32, BF16 = jnp.float32, jnp.bfloat16

PC = 50
ROWS = 56
SEC = 64
TILE = 2048
BLK = 512
HALF = TILE // 2
SPT = 128
RB = 256
blur = 0.25
LOG2E = math.log2(math.e)
SCALE = LOG2E / blur
UNSCALE = blur / LOG2E


def pieces3(v):
    one = v.astype(BF16).astype(F32)
    rest = v - one
    two = rest.astype(BF16).astype(F32)
    return one, two, (rest - two).astype(BF16).astype(F32)


def pad_rows(v, rows):
    return jnp.concatenate([v, jnp.zeros((rows - v.shape[0], v.shape[1]), v.dtype)], axis=0)


def lse(v, axis):
    top = jnp.max(v, axis=axis, keepdims=True)
    out = top + jnp.log2(jnp.sum(jnp.exp2(v - top), axis=axis, keepdims=True))
    return out


def kernel(
    cells_ref, spots_ref, loga_ref, logb_ref, outf_ref, outg_ref, outb_ref,
    cg, lab, lbb, sg, ab, bb, at, e, run, ucol, urow, rb1, rb2, cs1, cr1, cz1, gh1, cs2, cr2, cz2, gh2, gbuf, stage, rs, ag,
    pot, fo, tops, sums, qrow, ptb, bt, xsum,
    l_in, s_cell, r_cell, s_half, r_half, s_lab, r_lab, s_spot, r_spot, s_core, r_core, s_row1, r_row1, s_row2, r_row2,
    s_pair, r_pair, s_col1, r_col1, s_col2, r_col2, s_g, r_g, s_rs, r_rs, s_ag, r_ag, l_out,
):
    b = lax.axis_index("cell")
    x = lax.axis_index("spot")
    s = b & 15
    y, z, c = b // 16, s // 2, b & 1
    xy = x * 4 + y

    def dev(dx, dy, dz, dc):
        px, py, pz, pc = (x + dx) & 3, (y + dy) & 3, (z + dz) & 7, (c + dc) & 1
        return ((py * 8 + pz) * 2 + pc, px)

    row_peers = [(dx, dy, 0, 0) for dx in (2, 1, 3, 0) for dy in (2, 1, 3, 0) if dx or dy]
    ring = (4, 3, 5, 2, 6, 1, 7)
    ring_peers = [(0, 0, dz, 0) for dz in ring]
    sibling = (0, 0, 0, 1)
    peers = row_peers + ring_peers + [sibling]
    barrier = pltpu.get_barrier_semaphore()
    for peer in peers:
        pl.semaphore_signal(barrier, inc=1, device_id=dev(*peer), device_id_type=MESH)

    loads = [
        pltpu.make_async_copy(cells_ref.at[:, pl.ds(0, 256)], cg.at[y, 0], l_in.at[0]),
        pltpu.make_async_copy(cells_ref.at[:, pl.ds(256, 256)], cg.at[y, 1], l_in.at[1]),
        pltpu.make_async_copy(spots_ref, sg.at[s], l_in.at[2]),
        pltpu.make_async_copy(loga_ref, lab.at[y], l_in.at[3]),
        pltpu.make_async_copy(logb_ref.at[:, pl.ds(pl.multiple_of(y * TILE, TILE), TILE)], lbb, l_in.at[4]),
    ]
    for one in loads:
        one.start()
    run[0:8, :] = jnp.full((8, TILE), -jnp.inf, F32)
    run[8:16, :] = jnp.zeros((8, TILE), F32)
    for one in loads:
        one.wait()
    pl.semaphore_wait(barrier, len(peers))

    sends = []

    def copy(src, dst, ssem, rsem, peer):
        return pltpu.make_async_remote_copy(
            src_ref=src, dst_ref=dst, send_sem=ssem, recv_sem=rsem, device_id=dev(*peer), device_id_type=MESH
        )

    def start(*args):
        one = copy(*args)
        one.start()
        sends.append(one)
        return one

    def arrive(copies):
        for one in copies:
            one.wait_recv()

    near = {}
    for dy in (1, 3):
        for h in (0, 1) if dy == 1 else (1, 0):
            ref = cg.at[y, h]
            near[dy, h] = start(ref, ref, s_cell.at[dy, h], r_cell.at[dy, h], (0, dy, 0, 0))

    def turn(p):
        return jnp.where((p & 1) == 1, (p + 1) // 2, 8 - p // 2)

    def slot_of(p, other):
        return ((z + 8 - turn(p)) & 7) * 2 + (1 - c if other else c)

    def ring_copy(p):
        ref = sg.at[s]
        return copy(ref, ref, s_spot.at[p], r_spot.at[p], (0, 0, turn(p), 0))

    def hand_on(p):
        ref = sg.at[slot_of(p, False)]
        return copy(ref, ref, s_core.at[p], r_core.at[p], sibling)

    own = sg.at[s]
    pair0 = start(own, own, s_core.at[0], r_core.at[0], sibling)
    lax.fori_loop(1, 8, lambda p, carry: (ring_copy(p).start(), carry)[1], 0)
    lab_in = [start(lab.at[y], lab.at[y], s_lab.at[dy], r_lab.at[dy], (0, dy, 0, 0)) for dy in (1, 2, 3)]

    row = lax.broadcasted_iota(jnp.int32, (ROWS, 1), 0)
    centre = jnp.sum(sg[s], axis=1, keepdims=True) * (1.0 / SPT)

    def stack(v, extra, order):
        hi = v.astype(BF16)
        lo = (v - hi.astype(F32)).astype(BF16)
        first = pad_rows((hi.astype(F32) + extra).astype(BF16), SEC)
        hi, lo = pad_rows(hi, SEC), pad_rows(lo, SEC)
        return jnp.concatenate([first] + [(hi, lo)[k] for k in order], axis=0)

    def prep_cells(yy, h):
        lanes = pl.ds(pl.multiple_of(yy * BLK + h * 256, 256), 256)
        v = pad_rows(cg[yy, h] - centre, ROWS)
        pot[0:1, lanes] = jnp.sum(v * v, axis=0, keepdims=True) * SCALE
        extra = jnp.where((row >= PC) & (row < PC + 3), 1.0, 0.0) + jnp.zeros((ROWS, 256), F32)
        ab[:, lanes] = stack(v * (2.0 * SCALE), extra, (0, 1, 1))

    def prep_spots(slot):
        v = pad_rows(sg[slot] - centre, ROWS)
        norm = jnp.sum(v * v, axis=0, keepdims=True) * (-SCALE)
        n1, n2, n3 = pieces3(norm)
        extra = jnp.where(row == PC, n1, 0.0) + jnp.where(row == PC + 1, n2, 0.0) + jnp.where(row == PC + 2, n3, 0.0)
        extra = extra + jnp.where((row >= PC + 3) & (row < PC + 6), 1.0, 0.0)
        block = stack(v, extra, (1, 0, 1))
        bb[:, pl.ds(pl.multiple_of(slot * SPT, SPT), SPT)] = block
        bt[pl.ds(pl.multiple_of(slot * SPT, SPT), SPT), :] = block.T

    def update(slot, yy):
        lanes = pl.ds(pl.multiple_of(yy * BLK, BLK), BLK)
        left = bt[pl.ds(pl.multiple_of(slot * SPT, SPT), SPT), :]
        t = jnp.dot(left, ab[:, lanes], preferred_element_type=F32).reshape(SPT // 8, 8, BLK)
        old = run[0:8, lanes]
        top = jnp.maximum(old, jnp.max(t, axis=0))
        run[8:16, lanes] = run[8:16, lanes] * jnp.exp2(old - top) + jnp.sum(jnp.exp2(t - top[None]), axis=0)
        run[0:8, lanes] = top

    def stream(slots, offsets, fresh=True):
        if fresh:
            for slot in slots:
                prep_spots(slot)
        for slot in slots:
            for dy in offsets:
                update(slot, (y + dy) & 3)

    def got(p):
        ring_copy(p).wait_recv()
        hand_on(p).start()

    prep_cells(y, 0)
    prep_cells(y, 1)
    below, above = (y + 3) & 3, (y + 1) & 3
    near[1, 0].wait_recv()
    ref = cg.at[below, 0]
    far0 = start(ref, ref, s_half.at[0], r_half.at[0], (0, 1, 0, 0))
    near[3, 1].wait_recv()
    ref = cg.at[above, 1]
    far1 = start(ref, ref, s_half.at[1], r_half.at[1], (0, 3, 0, 0))
    prep_cells(below, 0)
    prep_cells(above, 1)
    near[1, 1].wait_recv()
    prep_cells(below, 1)
    near[3, 0].wait_recv()
    prep_cells(above, 0)

    got(1)
    got(2)
    pair0.wait_recv()
    stream([s, z * 2 + 1 - c, slot_of(1, False), slot_of(2, False)], (0, 1, 3))

    def four(k, carry):
        got(2 * k + 1)
        got(2 * k + 2)
        hand_on(2 * k - 1).wait_recv()
        hand_on(2 * k).wait_recv()
        stream(
            [slot_of(2 * k - 1, True), slot_of(2 * k, True), slot_of(2 * k + 1, False), slot_of(2 * k + 2, False)],
            (0, 1, 3),
        )
        return carry

    lax.fori_loop(1, 3, four, 0)
    arrive([far0, far1])
    yy = (y + 2) & 3
    prep_cells(yy, 0)
    prep_cells(yy, 1)
    stream([s, z * 2 + 1 - c] + [slot_of(p, False) for p in (1, 2, 3, 4)], (2,), False)
    got(7)
    stream([slot_of(p, True) for p in (1, 2, 3, 4)] + [slot_of(p, False) for p in (5, 6)], (2,), False)
    hand_on(5).wait_recv()
    hand_on(6).wait_recv()
    stream([slot_of(7, False), slot_of(5, True), slot_of(6, True)], (0, 1, 3, 2))
    hand_on(7).wait_recv()
    stream([slot_of(7, True)], (0, 1, 3, 2))
    top = jnp.max(run[0:8, :], axis=0, keepdims=True)
    total = jnp.sum(run[8:16, :] * jnp.exp2(run[0:8, :] - top), axis=0, keepdims=True)
    rb1[xy] = top + jnp.log2(total) - pot[0:1, :]

    def row_exchange(buf, ssem, rsem):
        return [start(buf.at[xy], buf.at[xy], ssem.at[k], rsem.at[k], peer) for k, peer in enumerate(row_peers)]

    moving = row_exchange(rb1, s_row1, r_row1)
    for k in range(TILE // 256):
        at[k * 256 : (k + 1) * 256, :] = ab[:, k * 256 : (k + 1) * 256].T
    arrive(lab_in)
    for k in range(4):
        pot[1:2, k * BLK : (k + 1) * BLK] = lab[k] * LOG2E
    arrive(moving)
    cell1 = pot[1:2, :] - lse(rb1[...], 0)[0]
    pot[2:3, :] = cell1
    f1, f2, f3 = pieces3(cell1 - pot[0:1, :])
    urow[0:1, :] = f1
    urow[1:2, :] = f2
    urow[2:3, :] = f3
    urow[3:8, :] = jnp.zeros((5, TILE), F32)
    lane = lax.broadcasted_iota(jnp.int32, (8, 128), 1)
    sub = lax.broadcasted_iota(jnp.int32, (8, 128), 0)
    pick = jnp.where((lane == sub + PC + 3) & (sub < 3), 1.0, 0.0)
    spread = lax.dot_general(
        urow[...].astype(BF16), pick.astype(BF16), (((0,), (0,)), ((), ())), preferred_element_type=F32
    )
    at[:, 0:128] = (at[:, 0:128].astype(F32) + spread).astype(BF16)

    def half_lanes(h):
        return pl.ds(pl.multiple_of(h * HALF, HALF), HALF)

    def col_pass(h):
        lanes = half_lanes(h)
        right = bb[:, lanes]
        for r in range(TILE // RB):
            t = jnp.dot(at[r * RB : (r + 1) * RB, :], right, preferred_element_type=F32)
            top = jnp.max(jnp.max(t.reshape(RB // 8, 8, HALF), axis=0), axis=0, keepdims=True)
            w = jnp.exp2(t - top)
            e[h, r * RB : (r + 1) * RB, :] = w
            tops[r : r + 1, lanes] = top
            sums[r : r + 1, lanes] = jnp.sum(jnp.sum(w.reshape(RB // 8, 8, HALF), axis=0), axis=0, keepdims=True)
        return lse(tops[:, lanes] + jnp.log2(sums[:, lanes]), 0)

    def ring_exchange(buf, ssem, rsem):
        return [start(buf.at[z], buf.at[z], ssem.at[k], rsem.at[k], peer) for k, peer in enumerate(ring_peers)]

    cs1[...] = col_pass(1 - c)
    half = start(cs1, cr1, s_pair.at[0], r_pair.at[0], sibling)
    mine = col_pass(c)
    half.wait_recv()
    cz1[z] = lse(jnp.concatenate([mine, cr1[...]], axis=0), 0)
    arrive(ring_exchange(cz1, s_col1, r_col1))
    gh1[c] = lbb[:, half_lanes(c)] * LOG2E - lse(cz1[...], 0)[0]
    back = start(gh1.at[c], gh1.at[c], s_pair.at[1], r_pair.at[1], sibling)

    def scales(h):
        q = jnp.exp2(tops[:, half_lanes(h)] + gh1[h])
        for r in range(TILE // RB):
            qrow[h, r] = q[r : r + 1]

    def row_sums(h, last):
        def step(r, carry):
            for k in (0, 1):
                rows = pl.ds(pl.multiple_of(r * RB + k * 128, 128), 128)
                t = ucol[rows, :] if last else jnp.zeros((128, 128), F32)
                for j in range(HALF // 128):
                    lanes = slice(j * 128, (j + 1) * 128)
                    w = e[h, rows, lanes] * qrow[h, r, :, lanes]
                    e[h, rows, lanes] = w
                    t = t + w
                if last:
                    rb2[xy, :, rows] = jnp.sum(t.T, axis=0, keepdims=True)
                else:
                    ucol[rows, :] = t
            return carry

        lax.fori_loop(0, TILE // RB, step, 0)

    scales(c)
    row_sums(c, False)
    back.wait_recv()
    scales(1 - c)
    row_sums(1 - c, True)
    arrive(row_exchange(rb2, s_row2, r_row2))
    ratio = jnp.exp2(pot[1:2, :]) / jnp.sum(rb2[...], axis=0)
    u1, u2, u3 = pieces3(ratio)
    urow[0:1, :] = u1
    urow[1:2, :] = u2
    urow[2:3, :] = u3
    ones = jnp.where(sub < 3, 1.0, 0.0)
    ucol[...] = lax.dot_general(
        urow[...].astype(BF16), ones.astype(BF16), (((0,), (0,)), ((), ())), preferred_element_type=F32
    )

    def col_sums(h):
        def step(r, t):
            out = list(t)
            for q in range(8):
                rows = pl.ds(pl.multiple_of(r * 64 + q * 8, 8), 8)
                scale = ucol[rows, :]
                for k in range(HALF // 128):
                    out[k] = out[k] + e[h, rows, k * 128 : (k + 1) * 128] * scale
            return tuple(out)

        parts = lax.fori_loop(0, TILE // 64, step, tuple(jnp.zeros((8, 128), F32) for k in range(HALF // 128)))
        return jnp.sum(jnp.concatenate(parts, axis=1), axis=0, keepdims=True)

    cs2[...] = col_sums(1 - c)
    half = start(cs2, cr2, s_pair.at[2], r_pair.at[2], sibling)
    mine = col_sums(c)
    half.wait_recv()
    cz2[z] = mine + cr2[...]
    moving = ring_exchange(cz2, s_col2, r_col2)
    fo[...] = (pot[2:3, :] + jnp.log2(ratio)) * UNSCALE
    out_f = pltpu.make_async_copy(fo.at[:, pl.ds(pl.multiple_of(y * BLK, BLK), BLK)], outf_ref, l_out.at[0])
    out_f.start()
    arrive(moving)
    gh2[c] = jnp.exp2(lbb[:, half_lanes(c)] * LOG2E) / jnp.sum(cz2[...], axis=0)
    back = start(gh2.at[c], gh2.at[c], s_pair.at[3], r_pair.at[3], sibling)

    def weigh(h):
        for k in range(8):
            lanes = slice(k * SPT, (k + 1) * SPT)
            v = jnp.where(row == PC, 1.0, pad_rows(sg[h * 8 + k], ROWS)) * gh2[h, :, lanes]
            hi = v.astype(BF16)
            ptb[h, 0:SEC, lanes] = pad_rows(hi, SEC)
            ptb[h, SEC : 2 * SEC, lanes] = pad_rows((v - hi.astype(F32)).astype(BF16), SEC)

    contract = (((1,), (1,)), ((), ()))

    def product(dy, h):
        w = e[h, pl.ds(pl.multiple_of(((y + dy) & 3) * BLK, BLK), BLK), :]
        hi = w.astype(BF16)
        lo = (w - hi.astype(F32)).astype(BF16)
        part = lax.dot_general(hi, ptb[h], contract, preferred_element_type=F32)
        return part + lax.dot_general(lo, ptb[h], contract, preferred_element_type=F32)

    along_x, along_y, g_in = {}, [], []

    def send_x(dy, part):
        part = part.T
        part = (part[0:ROWS] + part[SEC : SEC + ROWS])[0 : PC + 1]
        for k in range(4):
            stage[dy * 4 + k] = part[:, k * SPT : (k + 1) * SPT]
        along_x[dy] = []
        for dx in (2, 1, 3):
            k = dy * 4 + dx
            src, dst = stage.at[dy * 4 + ((x + dx) & 3)], rs.at[k]
            along_x[dy].append(start(src, dst, s_rs.at[k], r_rs.at[k], (dx, 0, 0, 0)))

    def send_y(dy):
        arrive(along_x[dy])
        k = dy * 4
        xsum[dy] = (stage[k + x] + rs[k + 1]) + (rs[k + 2] + rs[k + 3])
        if dy:
            along_y.append(start(xsum.at[dy], rs.at[k], s_rs.at[k], r_rs.at[k], (0, dy, 0, 0)))

    weigh(c)
    first = product(2, c)
    back.wait_recv()
    weigh(1 - c)
    send_x(2, first + product(2, 1 - c))
    for h in (0, 1):
        gbuf[y, :, h * HALF : (h + 1) * HALF] = (gh1[h] + jnp.log2(gh2[h])) * UNSCALE
    send_x(1, product(1, c) + product(1, 1 - c))
    send_x(3, product(3, c) + product(3, 1 - c))
    send_y(2)
    send_x(0, product(0, c) + product(0, 1 - c))
    for dy in (2, 1, 3):
        g_in.append(start(gbuf.at[y], gbuf.at[y], s_g.at[dy], r_g.at[dy], (0, dy, 0, 0)))
    send_y(1)
    send_y(3)
    send_y(0)
    arrive(g_in)
    outs = [
        pltpu.make_async_copy(gbuf.at[k], outg_ref.at[:, pl.ds(k * TILE, TILE)], l_out.at[1 + k]) for k in range(4)
    ]
    for one in outs:
        one.start()
    arrive(along_y)
    whole = (xsum[0] + rs[4]) + (rs[8] + rs[12])
    ag[x] = whole[0:PC] / whole[PC : PC + 1, :]
    mine = ag.at[x]
    ag_in = [start(mine, mine, s_ag.at[dx], r_ag.at[dx], (dx, 0, 0, 0)) for dx in (2, 1, 3)]
    arrive(ag_in)
    for k in range(4):
        outs.append(
            pltpu.make_async_copy(ag.at[k], outb_ref.at[:, pl.ds(k * SPT, SPT)], l_out.at[5 + k])
        )
        outs[-1].start()
    for one in sends:
        one.wait_send()

    def drain(p, carry):
        ring_copy(p).wait_send()
        hand_on(p).wait_send()
        return carry

    lax.fori_loop(1, 8, drain, 0)
    for one in [out_f] + outs:
        one.wait()


def settle(f_ref, g_ref, b_ref, outf_ref, outg_ref, outb_ref):
    outf_ref[...] = f_ref[...]
    outg_ref[...] = g_ref[...]
    outb_ref[...] = b_ref[...]


def on_device(cells_pca, spots_pca, log_a, log_b):
    dma = pltpu.SemaphoreType.DMA
    hbm = pl.BlockSpec(memory_space=pl.ANY)
    vmem = pl.BlockSpec(memory_space=pltpu.VMEM)
    shapes = (
        jax.ShapeDtypeStruct((1, BLK), F32),
        jax.ShapeDtypeStruct((1, 4 * TILE), F32),
        jax.ShapeDtypeStruct((PC, BLK), F32),
    )
    pairs = ((4, 2), (2,), (4,), (8,), (8,), (15,), (15,), (4,), (7,), (7,), (4,), (16,), (4,))
    out = pl.pallas_call(
        kernel,
        out_shape=shapes,
        in_specs=[hbm] * 4,
        out_specs=(hbm,) * 3,
        scratch_shapes=[
            pltpu.VMEM((4, 2, PC, 256), F32),
            pltpu.VMEM((4, 1, BLK), F32),
            pltpu.VMEM((1, TILE), F32),
            pltpu.VMEM((16, PC, SPT), F32),
            pltpu.VMEM((4 * SEC, TILE), BF16),
            pltpu.VMEM((4 * SEC, TILE), BF16),
            pltpu.VMEM((TILE, 4 * SEC), BF16),
            pltpu.VMEM((2, TILE, HALF), F32),
            pltpu.VMEM((16, TILE), F32),
            pltpu.VMEM((TILE, 128), F32),
            pltpu.VMEM((8, TILE), F32),
            pltpu.VMEM((16, 1, TILE), F32),
            pltpu.VMEM((16, 1, TILE), F32),
            pltpu.VMEM((1, HALF), F32),
            pltpu.VMEM((1, HALF), F32),
            pltpu.VMEM((8, 1, HALF), F32),
            pltpu.VMEM((2, 1, HALF), F32),
            pltpu.VMEM((1, HALF), F32),
            pltpu.VMEM((1, HALF), F32),
            pltpu.VMEM((8, 1, HALF), F32),
            pltpu.VMEM((2, 1, HALF), F32),
            pltpu.VMEM((4, 1, TILE), F32),
            pltpu.VMEM((16, PC + 1, SPT), F32),
            pltpu.VMEM((16, PC + 1, SPT), F32),
            pltpu.VMEM((4, PC, SPT), F32),
            pltpu.VMEM((8, TILE), F32),
            pltpu.VMEM((1, TILE), F32),
            pltpu.VMEM((TILE // RB, TILE), F32),
            pltpu.VMEM((TILE // RB, TILE), F32),
            pltpu.VMEM((2, TILE // RB, 1, HALF), F32),
            pltpu.VMEM((2, 2 * SEC, HALF), BF16),
            pltpu.VMEM((TILE, 4 * SEC), BF16),
            pltpu.VMEM((4, PC + 1, SPT), F32),
            dma((5,)),
        ]
        + [dma(n) for n in pairs for _ in range(2)]
        + [dma((9,))],
        compiler_params=pltpu.CompilerParams(
            collective_id=0, has_side_effects=True, vmem_limit_bytes=58 * 2**20
        ),
        cost_estimate=pl.CostEstimate(flops=10 * 2**30, bytes_accessed=2**20, transcendentals=2**23),
        name="sinkhorn",
    )(cells_pca, spots_pca, log_a.reshape(1, BLK), log_b.reshape(1, 4 * TILE))
    f, g, bary = pl.pallas_call(
        settle,
        out_shape=shapes,
        in_specs=[vmem] * 3,
        out_specs=(vmem,) * 3,
        name="settle",
    )(*out)
    return f.reshape(BLK), g.reshape(4 * TILE), bary


def solution(mesh):
    placed = (P(None, "cell"), P(None, ("spot", "cell")), P("cell"), P("spot"))
    return jax.shard_map(
        on_device,
        mesh=mesh,
        in_specs=placed,
        out_specs=(P("cell"), P("spot"), P(None, "cell")),
        check_vma=False,
    )
```

```python
import math

import jax
import jax.numpy as jnp
from jax import lax
from jax.experimental import pallas as pl
from jax.experimental.pallas import tpu as pltpu
from jax.sharding import PartitionSpec as P

MESH = pl.DeviceIdType.MESH
F32, BF16 = jnp.float32, jnp.bfloat16

PC = 50
ROWS = 56
SEC = 64
TILE = 2048
BLK = 512
HALF = TILE // 2
SPT = 128
RB = 128
blur = 0.25
LOG2E = math.log2(math.e)
SCALE = LOG2E / blur
UNSCALE = blur / LOG2E


def pieces3(v):
    one = v.astype(BF16).astype(F32)
    rest = v - one
    two = rest.astype(BF16).astype(F32)
    return one, two, (rest - two).astype(BF16).astype(F32)


def pad_rows(v, rows):
    return jnp.concatenate([v, jnp.zeros((rows - v.shape[0], v.shape[1]), v.dtype)], axis=0)


def lse(v, axis):
    top = jnp.max(v, axis=axis, keepdims=True)
    out = top + jnp.log2(jnp.sum(jnp.exp2(v - top), axis=axis, keepdims=True))
    return out


def kernel(
    cells_ref, spots_ref, loga_ref, logb_ref, outf_ref, outg_ref, outb_ref,
    cg, lab, lbb, sg, ab, bb, at, e, run, ucol, urow, rb1, rb2, cs1, cr1, cz1, gh1, cs2, cr2, cz2, gh2, gbuf, stage, rs, ag,
    pot, fo, tops, sums, qrow, ptb, eh, el, bt, xsum,
    l_in, s_cell, r_cell, s_half, r_half, s_lab, r_lab, s_spot, r_spot, s_core, r_core, s_row1, r_row1, s_row2, r_row2,
    s_pair, r_pair, s_col1, r_col1, s_col2, r_col2, s_g, r_g, s_rs, r_rs, s_ag, r_ag, l_out,
):
    b = lax.axis_index("cell")
    x = lax.axis_index("spot")
    s = b & 15
    y, z, c = b // 16, s // 2, b & 1
    xy = x * 4 + y

    def dev(dx, dy, dz, dc):
        px, py, pz, pc = (x + dx) & 3, (y + dy) & 3, (z + dz) & 7, (c + dc) & 1
        return ((py * 8 + pz) * 2 + pc, px)

    row_peers = [(dx, dy, 0, 0) for dx in (2, 1, 3, 0) for dy in (2, 1, 3, 0) if dx or dy]
    ring = (4, 3, 5, 2, 6, 1, 7)
    ring_peers = [(0, 0, dz, 0) for dz in ring]
    sibling = (0, 0, 0, 1)
    peers = row_peers + ring_peers + [sibling]
    barrier = pltpu.get_barrier_semaphore()
    for peer in peers:
        pl.semaphore_signal(barrier, inc=1, device_id=dev(*peer), device_id_type=MESH)

    loads = [
        pltpu.make_async_copy(cells_ref.at[:, pl.ds(0, 256)], cg.at[y, 0], l_in.at[0]),
        pltpu.make_async_copy(cells_ref.at[:, pl.ds(256, 256)], cg.at[y, 1], l_in.at[1]),
        pltpu.make_async_copy(spots_ref, sg.at[s], l_in.at[2]),
        pltpu.make_async_copy(loga_ref, lab.at[y], l_in.at[3]),
        pltpu.make_async_copy(logb_ref.at[:, pl.ds(pl.multiple_of(y * TILE, TILE), TILE)], lbb, l_in.at[4]),
    ]
    for one in loads:
        one.start()
    run[0:8, :] = jnp.full((8, TILE), -jnp.inf, F32)
    run[8:16, :] = jnp.zeros((8, TILE), F32)
    for one in loads:
        one.wait()
    pl.semaphore_wait(barrier, len(peers))

    sends = []

    def copy(src, dst, ssem, rsem, peer):
        return pltpu.make_async_remote_copy(
            src_ref=src, dst_ref=dst, send_sem=ssem, recv_sem=rsem, device_id=dev(*peer), device_id_type=MESH
        )

    def start(*args):
        one = copy(*args)
        one.start()
        sends.append(one)
        return one

    def arrive(copies):
        for one in copies:
            one.wait_recv()

    near = {}
    for dy in (1, 3):
        for h in (0, 1) if dy == 1 else (1, 0):
            ref = cg.at[y, h]
            near[dy, h] = start(ref, ref, s_cell.at[dy, h], r_cell.at[dy, h], (0, dy, 0, 0))

    def turn(p):
        return jnp.where((p & 1) == 1, (p + 1) // 2, 8 - p // 2)

    def slot_of(p, other):
        return ((z + 8 - turn(p)) & 7) * 2 + (1 - c if other else c)

    def ring_copy(p):
        ref = sg.at[s]
        return copy(ref, ref, s_spot.at[p], r_spot.at[p], (0, 0, turn(p), 0))

    def hand_on(p):
        ref = sg.at[slot_of(p, False)]
        return copy(ref, ref, s_core.at[p], r_core.at[p], sibling)

    own = sg.at[s]
    pair0 = start(own, own, s_core.at[0], r_core.at[0], sibling)
    lax.fori_loop(1, 8, lambda p, carry: (ring_copy(p).start(), carry)[1], 0)
    lab_in = [start(lab.at[y], lab.at[y], s_lab.at[dy], r_lab.at[dy], (0, dy, 0, 0)) for dy in (1, 2, 3)]

    row = lax.broadcasted_iota(jnp.int32, (ROWS, 1), 0)
    centre = jnp.sum(sg[s], axis=1, keepdims=True) * (1.0 / SPT)

    def stack(v, extra, order):
        hi = v.astype(BF16)
        lo = (v - hi.astype(F32)).astype(BF16)
        first = pad_rows((hi.astype(F32) + extra).astype(BF16), SEC)
        hi, lo = pad_rows(hi, SEC), pad_rows(lo, SEC)
        return jnp.concatenate([first] + [(hi, lo)[k] for k in order], axis=0)

    def prep_cells(yy, h):
        lanes = pl.ds(pl.multiple_of(yy * BLK + h * 256, 256), 256)
        v = pad_rows(cg[yy, h] - centre, ROWS)
        pot[0:1, lanes] = jnp.sum(v * v, axis=0, keepdims=True) * SCALE
        extra = jnp.where((row >= PC) & (row < PC + 3), 1.0, 0.0) + jnp.zeros((ROWS, 256), F32)
        ab[:, lanes] = stack(v * (2.0 * SCALE), extra, (0, 1, 1))

    def prep_spots(slot):
        v = pad_rows(sg[slot] - centre, ROWS)
        norm = jnp.sum(v * v, axis=0, keepdims=True) * (-SCALE)
        n1, n2, n3 = pieces3(norm)
        extra = jnp.where(row == PC, n1, 0.0) + jnp.where(row == PC + 1, n2, 0.0) + jnp.where(row == PC + 2, n3, 0.0)
        extra = extra + jnp.where((row >= PC + 3) & (row < PC + 6), 1.0, 0.0)
        block = stack(v, extra, (1, 0, 1))
        bb[:, pl.ds(pl.multiple_of(slot * SPT, SPT), SPT)] = block
        bt[pl.ds(pl.multiple_of(slot * SPT, SPT), SPT), :] = block.T

    def update(slot, yy):
        lanes = pl.ds(pl.multiple_of(yy * BLK, BLK), BLK)
        left = bt[pl.ds(pl.multiple_of(slot * SPT, SPT), SPT), :]
        t = jnp.dot(left, ab[:, lanes], preferred_element_type=F32).reshape(SPT // 8, 8, BLK)
        old = run[0:8, lanes]
        top = jnp.maximum(old, jnp.max(t, axis=0))
        run[8:16, lanes] = run[8:16, lanes] * jnp.exp2(old - top) + jnp.sum(jnp.exp2(t - top[None]), axis=0)
        run[0:8, lanes] = top

    def stream(slots, offsets, fresh=True):
        if fresh:
            for slot in slots:
                prep_spots(slot)
        for slot in slots:
            for dy in offsets:
                update(slot, (y + dy) & 3)

    def got(p):
        ring_copy(p).wait_recv()
        hand_on(p).start()

    prep_cells(y, 0)
    prep_cells(y, 1)
    below, above = (y + 3) & 3, (y + 1) & 3
    near[1, 0].wait_recv()
    ref = cg.at[below, 0]
    far0 = start(ref, ref, s_half.at[0], r_half.at[0], (0, 1, 0, 0))
    near[3, 1].wait_recv()
    ref = cg.at[above, 1]
    far1 = start(ref, ref, s_half.at[1], r_half.at[1], (0, 3, 0, 0))
    prep_cells(below, 0)
    prep_cells(above, 1)
    near[1, 1].wait_recv()
    prep_cells(below, 1)
    near[3, 0].wait_recv()
    prep_cells(above, 0)

    got(1)
    got(2)
    pair0.wait_recv()
    stream([s, z * 2 + 1 - c, slot_of(1, False), slot_of(2, False)], (0, 1, 3))

    def four(k, carry):
        got(2 * k + 1)
        got(2 * k + 2)
        hand_on(2 * k - 1).wait_recv()
        hand_on(2 * k).wait_recv()
        stream(
            [slot_of(2 * k - 1, True), slot_of(2 * k, True), slot_of(2 * k + 1, False), slot_of(2 * k + 2, False)],
            (0, 1, 3),
        )
        return carry

    lax.fori_loop(1, 3, four, 0)
    arrive([far0, far1])
    yy = (y + 2) & 3
    prep_cells(yy, 0)
    prep_cells(yy, 1)
    stream([s, z * 2 + 1 - c] + [slot_of(p, False) for p in (1, 2, 3, 4)], (2,), False)
    got(7)
    stream([slot_of(p, True) for p in (1, 2, 3, 4)] + [slot_of(p, False) for p in (5, 6)], (2,), False)
    hand_on(5).wait_recv()
    hand_on(6).wait_recv()
    stream([slot_of(7, False), slot_of(5, True), slot_of(6, True)], (0, 1, 3, 2))
    hand_on(7).wait_recv()
    stream([slot_of(7, True)], (0, 1, 3, 2))
    top = jnp.max(run[0:8, :], axis=0, keepdims=True)
    total = jnp.sum(run[8:16, :] * jnp.exp2(run[0:8, :] - top), axis=0, keepdims=True)
    rb1[xy] = top + jnp.log2(total) - pot[0:1, :]

    def row_exchange(buf, ssem, rsem):
        return [start(buf.at[xy], buf.at[xy], ssem.at[k], rsem.at[k], peer) for k, peer in enumerate(row_peers)]

    moving = row_exchange(rb1, s_row1, r_row1)
    for k in range(TILE // 256):
        at[k * 256 : (k + 1) * 256, :] = ab[:, k * 256 : (k + 1) * 256].T
    for h in (0, 1):
        for r in range(TILE // 256):
            rows = slice(r * 256, (r + 1) * 256)
            e[h, rows, :] = jnp.dot(at[rows, :], bb[:, h * HALF : (h + 1) * HALF], preferred_element_type=F32)
    arrive(lab_in)
    for k in range(4):
        pot[1:2, k * BLK : (k + 1) * BLK] = lab[k] * LOG2E
    arrive(moving)
    cell1 = pot[1:2, :] - lse(rb1[...], 0)[0]
    pot[2:3, :] = cell1
    f1, f2, f3 = pieces3(cell1 - pot[0:1, :])
    urow[0:1, :] = f1
    urow[1:2, :] = f2
    urow[2:3, :] = f3
    urow[3:8, :] = jnp.zeros((5, TILE), F32)
    sub = lax.broadcasted_iota(jnp.int32, (8, 128), 0)
    ones = jnp.where(sub < 3, 1.0, 0.0).astype(BF16)

    def to_column():
        return lax.dot_general(
            urow[...].astype(BF16), ones, (((0,), (0,)), ((), ())), preferred_element_type=F32
        )

    ucol[...] = to_column()

    def half_lanes(h):
        return pl.ds(pl.multiple_of(h * HALF, HALF), HALF)

    def col_pass(h):
        def step(r, carry):
            for q in range(2):
                at_r = r * 2 + q
                rows = pl.ds(pl.multiple_of(at_r * RB, RB), RB)
                f = ucol[rows, :]
                for k in range(HALF // 128):
                    lanes = slice(k * 128, (k + 1) * 128)
                    v = (e[h, rows, lanes] + f).reshape(RB // 8, 8, 128)
                    top = jnp.max(v, axis=0)
                    w = jnp.exp2(v - top[None])
                    e[h, rows, lanes] = w.reshape(RB, 128)
                    tops[h, at_r, :, lanes] = top
                    sums[at_r, :, lanes] = jnp.sum(w, axis=0)
            return carry

        lax.fori_loop(0, TILE // 256, step, 0)
        part = tops[h].reshape(TILE // RB * 8, HALF)
        top = jnp.max(part, axis=0, keepdims=True)
        total = jnp.sum(sums[...].reshape(TILE // RB * 8, HALF) * jnp.exp2(part - top), axis=0, keepdims=True)
        return top + jnp.log2(total)

    def ring_exchange(buf, ssem, rsem):
        return [start(buf.at[z], buf.at[z], ssem.at[k], rsem.at[k], peer) for k, peer in enumerate(ring_peers)]

    cs1[...] = col_pass(1 - c)
    half = start(cs1, cr1, s_pair.at[0], r_pair.at[0], sibling)
    mine = col_pass(c)
    half.wait_recv()
    cz1[z] = lse(jnp.concatenate([mine, cr1[...]], axis=0), 0)
    arrive(ring_exchange(cz1, s_col1, r_col1))
    gh1[c] = lbb[:, half_lanes(c)] * LOG2E - lse(cz1[...], 0)[0]
    back = start(gh1.at[c], gh1.at[c], s_pair.at[1], r_pair.at[1], sibling)

    def scales(h):
        qrow[h] = jnp.exp2(tops[h] + gh1[h])

    def row_sums(h, last):
        def step(r, carry):
            q = [qrow[h, r, :, j * 128 : (j + 1) * 128] for j in range(HALF // 128)]
            block = pl.ds(pl.multiple_of(r * RB, RB), RB)
            before = ucol[block, :] if last else None
            out = []
            for g in range(RB // 8):
                rows = pl.ds(pl.multiple_of(r * RB + g * 8, 8), 8)
                t = [e[h, rows, j * 128 : (j + 1) * 128] * q[j] for j in range(HALF // 128)]
                while len(t) > 1:
                    t = [t[j] + t[j + 1] for j in range(0, len(t), 2)]
                out.append(t[0])
            out = jnp.concatenate(out, axis=0)
            ucol[block, :] = before + out if last else out
            return carry

        lax.fori_loop(0, TILE // RB, step, 0)

    def to_row():
        for k in range(TILE // 128):
            rows = slice(k * 128, (k + 1) * 128)
            rb2[xy, :, rows] = jnp.sum(ucol[rows, :].T, axis=0, keepdims=True)

    scales(c)
    row_sums(c, False)
    back.wait_recv()
    scales(1 - c)
    row_sums(1 - c, True)
    to_row()
    arrive(row_exchange(rb2, s_row2, r_row2))
    ratio = jnp.exp2(pot[1:2, :]) / jnp.sum(rb2[...], axis=0)
    u1, u2, u3 = pieces3(ratio)
    urow[0:1, :] = u1
    urow[1:2, :] = u2
    urow[2:3, :] = u3
    ucol[...] = to_column()

    def col_sums(h):
        def step(r, t):
            out = [jnp.zeros((8, 128), F32) for k in t]
            for g in range(RB // 8):
                rows = pl.ds(pl.multiple_of(r * RB + g * 8, 8), 8)
                scale = ucol[rows, :]
                for k in range(HALF // 128):
                    out[k] = out[k] + e[h, rows, k * 128 : (k + 1) * 128] * scale
            return tuple(t[k] + out[k] * qrow[h, r, :, k * 128 : (k + 1) * 128] for k in range(HALF // 128))

        parts = lax.fori_loop(0, TILE // RB, step, tuple(jnp.zeros((8, 128), F32) for k in range(HALF // 128)))
        return jnp.sum(jnp.concatenate(parts, axis=1), axis=0, keepdims=True)

    cs2[...] = col_sums(1 - c)
    half = start(cs2, cr2, s_pair.at[2], r_pair.at[2], sibling)
    mine = col_sums(c)
    half.wait_recv()
    cz2[z] = mine + cr2[...]
    moving = ring_exchange(cz2, s_col2, r_col2)
    fo[...] = (pot[2:3, :] + jnp.log2(ratio)) * UNSCALE
    out_f = pltpu.make_async_copy(fo.at[:, pl.ds(pl.multiple_of(y * BLK, BLK), BLK)], outf_ref, l_out.at[0])
    out_f.start()

    def halve(r, carry):
        rows = pl.ds(pl.multiple_of(r * RB, RB), RB)
        for h in (0, 1):
            for j in range(HALF // 256):
                lanes = slice(j * 256, (j + 1) * 256)
                w = (e[h, rows, lanes].reshape(RB // 8, 8, 256) * qrow[h, r, :, lanes][None]).reshape(RB, 256)
                hi = w.astype(BF16)
                eh[h, rows, lanes] = hi
                el[h, rows, lanes] = (w - hi.astype(F32)).astype(BF16)
        return carry

    lax.fori_loop(0, TILE // RB, halve, 0)
    arrive(moving)
    gh2[c] = jnp.exp2(lbb[:, half_lanes(c)] * LOG2E) / jnp.sum(cz2[...], axis=0)
    back = start(gh2.at[c], gh2.at[c], s_pair.at[3], r_pair.at[3], sibling)

    def weigh(h):
        for k in range(8):
            lanes = slice(k * SPT, (k + 1) * SPT)
            v = jnp.where(row == PC, 1.0, pad_rows(sg[h * 8 + k], ROWS)) * gh2[h, :, lanes]
            hi = v.astype(BF16)
            lo = (v - hi.astype(F32)).astype(BF16)
            ptb[h, lanes, :] = jnp.concatenate([pad_rows(hi, SEC), pad_rows(lo, SEC)], axis=0).T

    def product(dy, h):
        rows = pl.ds(pl.multiple_of(((y + dy) & 3) * BLK, BLK), BLK)
        part = jnp.dot(eh[h, rows, :], ptb[h], preferred_element_type=F32)
        return part + jnp.dot(el[h, rows, :], ptb[h], preferred_element_type=F32)

    along_x, along_y, g_in = {}, [], []

    def send_x(dy, part):
        part = part.T
        part = (part[0:ROWS] + part[SEC : SEC + ROWS])[0 : PC + 1]
        for k in range(4):
            stage[dy * 4 + k] = part[:, k * SPT : (k + 1) * SPT]
        along_x[dy] = []
        for dx in (2, 1, 3):
            k = dy * 4 + dx
            src, dst = stage.at[dy * 4 + ((x + dx) & 3)], rs.at[k]
            along_x[dy].append(start(src, dst, s_rs.at[k], r_rs.at[k], (dx, 0, 0, 0)))

    def send_y(dy):
        arrive(along_x[dy])
        k = dy * 4
        xsum[dy] = (stage[k + x] + rs[k + 1]) + (rs[k + 2] + rs[k + 3])
        if dy:
            along_y.append(start(xsum.at[dy], rs.at[k], s_rs.at[k], r_rs.at[k], (0, dy, 0, 0)))

    weigh(c)
    first = product(2, c)
    back.wait_recv()
    weigh(1 - c)
    first = first + product(2, 1 - c)
    second = product(1, c) + product(1, 1 - c)
    send_x(2, first)
    for h in (0, 1):
        gbuf[y, :, h * HALF : (h + 1) * HALF] = (gh1[h] + jnp.log2(gh2[h])) * UNSCALE
    third = product(3, c) + product(3, 1 - c)
    send_x(1, second)
    for dy in (2, 1, 3):
        g_in.append(start(gbuf.at[y], gbuf.at[y], s_g.at[dy], r_g.at[dy], (0, dy, 0, 0)))
    fourth = product(0, c) + product(0, 1 - c)
    send_x(3, third)
    send_x(0, fourth)
    send_y(2)
    send_y(1)
    send_y(3)
    send_y(0)
    arrive(g_in)
    outs = [
        pltpu.make_async_copy(gbuf.at[k], outg_ref.at[:, pl.ds(k * TILE, TILE)], l_out.at[1 + k]) for k in range(4)
    ]
    for one in outs:
        one.start()
    arrive(along_y)
    whole = (xsum[0] + rs[4]) + (rs[8] + rs[12])
    ag[x] = whole[0:PC] / whole[PC : PC + 1, :]
    mine = ag.at[x]
    ag_in = [start(mine, mine, s_ag.at[dx], r_ag.at[dx], (dx, 0, 0, 0)) for dx in (2, 1, 3)]
    arrive(ag_in)
    for k in range(4):
        outs.append(
            pltpu.make_async_copy(ag.at[k], outb_ref.at[:, pl.ds(k * SPT, SPT)], l_out.at[5 + k])
        )
        outs[-1].start()
    for one in sends:
        one.wait_send()

    def drain(p, carry):
        ring_copy(p).wait_send()
        hand_on(p).wait_send()
        return carry

    lax.fori_loop(1, 8, drain, 0)
    for one in [out_f] + outs:
        one.wait()


def settle(f_ref, g_ref, b_ref, outf_ref, outg_ref, outb_ref):
    outf_ref[...] = f_ref[...]
    outg_ref[...] = g_ref[...]
    outb_ref[...] = b_ref[...]


def on_device(cells_pca, spots_pca, log_a, log_b):
    dma = pltpu.SemaphoreType.DMA
    hbm = pl.BlockSpec(memory_space=pl.ANY)
    vmem = pl.BlockSpec(memory_space=pltpu.VMEM)
    shapes = (
        jax.ShapeDtypeStruct((1, BLK), F32),
        jax.ShapeDtypeStruct((1, 4 * TILE), F32),
        jax.ShapeDtypeStruct((PC, BLK), F32),
    )
    pairs = ((4, 2), (2,), (4,), (8,), (8,), (15,), (15,), (4,), (7,), (7,), (4,), (16,), (4,))
    out = pl.pallas_call(
        kernel,
        out_shape=shapes,
        in_specs=[hbm] * 4,
        out_specs=(hbm,) * 3,
        scratch_shapes=[
            pltpu.VMEM((4, 2, PC, 256), F32),
            pltpu.VMEM((4, 1, BLK), F32),
            pltpu.VMEM((1, TILE), F32),
            pltpu.VMEM((16, PC, SPT), F32),
            pltpu.VMEM((4 * SEC, TILE), BF16),
            pltpu.VMEM((4 * SEC, TILE), BF16),
            pltpu.VMEM((TILE, 4 * SEC), BF16),
            pltpu.VMEM((2, TILE, HALF), F32),
            pltpu.VMEM((16, TILE), F32),
            pltpu.VMEM((TILE, 128), F32),
            pltpu.VMEM((8, TILE), F32),
            pltpu.VMEM((16, 1, TILE), F32),
            pltpu.VMEM((16, 1, TILE), F32),
            pltpu.VMEM((1, HALF), F32),
            pltpu.VMEM((1, HALF), F32),
            pltpu.VMEM((8, 1, HALF), F32),
            pltpu.VMEM((2, 1, HALF), F32),
            pltpu.VMEM((1, HALF), F32),
            pltpu.VMEM((1, HALF), F32),
            pltpu.VMEM((8, 1, HALF), F32),
            pltpu.VMEM((2, 1, HALF), F32),
            pltpu.VMEM((4, 1, TILE), F32),
            pltpu.VMEM((16, PC + 1, SPT), F32),
            pltpu.VMEM((16, PC + 1, SPT), F32),
            pltpu.VMEM((4, PC, SPT), F32),
            pltpu.VMEM((8, TILE), F32),
            pltpu.VMEM((1, TILE), F32),
            pltpu.VMEM((2, TILE // RB, 8, HALF), F32),
            pltpu.VMEM((TILE // RB, 8, HALF), F32),
            pltpu.VMEM((2, TILE // RB, 8, HALF), F32),
            pltpu.VMEM((2, HALF, 2 * SEC), BF16),
            pltpu.VMEM((2, TILE, HALF), BF16),
            pltpu.VMEM((2, TILE, HALF), BF16),
            pltpu.VMEM((TILE, 4 * SEC), BF16),
            pltpu.VMEM((4, PC + 1, SPT), F32),
            dma((5,)),
        ]
        + [dma(n) for n in pairs for _ in range(2)]
        + [dma((9,))],
        compiler_params=pltpu.CompilerParams(
            collective_id=0, has_side_effects=True, vmem_limit_bytes=58 * 2**20
        ),
        cost_estimate=pl.CostEstimate(flops=10 * 2**30, bytes_accessed=2**20, transcendentals=2**23),
        name="sinkhorn",
    )(cells_pca, spots_pca, log_a.reshape(1, BLK), log_b.reshape(1, 4 * TILE))
    f, g, bary = pl.pallas_call(
        settle,
        out_shape=shapes,
        in_specs=[vmem] * 3,
        out_specs=(vmem,) * 3,
        name="settle",
    )(*out)
    return f.reshape(BLK), g.reshape(4 * TILE), bary


def solution(mesh):
    placed = (P(None, "cell"), P(None, ("spot", "cell")), P("cell"), P("spot"))
    return jax.shard_map(
        on_device,
        mesh=mesh,
        in_specs=placed,
        out_specs=(P("cell"), P("spot"), P(None, "cell")),
        check_vma=False,
    )
```

```python
import math

import jax
import jax.numpy as jnp
from jax import lax
from jax.experimental import pallas as pl
from jax.experimental.pallas import tpu as pltpu
from jax.sharding import PartitionSpec as P

MESH = pl.DeviceIdType.MESH
F32, BF16 = jnp.float32, jnp.bfloat16

PC = 50
ROWS = 56
SEC = 64
TILE = 2048
BLK = 512
HALF = TILE // 2
SPT = 128
RB = 128
blur = 0.25
LOG2E = math.log2(math.e)
SCALE = LOG2E / blur
UNSCALE = blur / LOG2E


def pieces3(v):
    one = v.astype(BF16).astype(F32)
    rest = v - one
    two = rest.astype(BF16).astype(F32)
    return one, two, (rest - two).astype(BF16).astype(F32)


def pad_rows(v, rows):
    return jnp.concatenate([v, jnp.zeros((rows - v.shape[0], v.shape[1]), v.dtype)], axis=0)


def lse(v, axis):
    top = jnp.max(v, axis=axis, keepdims=True)
    out = top + jnp.log2(jnp.sum(jnp.exp2(v - top), axis=axis, keepdims=True))
    return out


def kernel(
    cells_ref, spots_ref, loga_ref, logb_ref, outf_ref, outg_ref, outb_ref,
    cg, lab, lbb, sg, ab, bb, at, e, run, ucol, urow, rb1, rb2, cs1, cr1, cz1, gh1, cs2, cr2, cz2, gh2, gbuf, stage, rs, ag,
    pot, fo, tops, sums, qrow, ptb, eh, el, bt, xsum,
    l_in, s_cell, r_cell, s_half, r_half, s_lab, r_lab, s_spot, r_spot, s_core, r_core, s_row1, r_row1, s_row2, r_row2,
    s_pair, r_pair, s_col1, r_col1, s_col2, r_col2, s_g, r_g, s_rs, r_rs, s_ag, r_ag, l_out,
):
    b = lax.axis_index("cell")
    x = lax.axis_index("spot")
    s = b & 15
    y, z, c = b // 16, s // 2, b & 1
    xy = x * 4 + y

    def dev(dx, dy, dz, dc):
        px, py, pz, pc = (x + dx) & 3, (y + dy) & 3, (z + dz) & 7, (c + dc) & 1
        return ((py * 8 + pz) * 2 + pc, px)

    row_peers = [(dx, dy, 0, 0) for dx in (2, 1, 3, 0) for dy in (2, 1, 3, 0) if dx or dy]
    ring = (4, 3, 5, 2, 6, 1, 7)
    ring_peers = [(0, 0, dz, 0) for dz in ring]
    sibling = (0, 0, 0, 1)
    peers = row_peers + ring_peers + [sibling]
    barrier = pltpu.get_barrier_semaphore()
    for peer in peers:
        pl.semaphore_signal(barrier, inc=1, device_id=dev(*peer), device_id_type=MESH)

    loads = [
        pltpu.make_async_copy(cells_ref.at[:, pl.ds(0, 256)], cg.at[y, 0], l_in.at[0]),
        pltpu.make_async_copy(cells_ref.at[:, pl.ds(256, 256)], cg.at[y, 1], l_in.at[1]),
        pltpu.make_async_copy(spots_ref, sg.at[s], l_in.at[2]),
        pltpu.make_async_copy(loga_ref, lab.at[y], l_in.at[3]),
        pltpu.make_async_copy(logb_ref.at[:, pl.ds(pl.multiple_of(y * TILE, TILE), TILE)], lbb, l_in.at[4]),
    ]
    for one in loads:
        one.start()
    run[0:8, :] = jnp.full((8, TILE), -jnp.inf, F32)
    run[8:16, :] = jnp.zeros((8, TILE), F32)
    for one in loads:
        one.wait()
    pl.semaphore_wait(barrier, len(peers))

    sends = []

    def copy(src, dst, ssem, rsem, peer):
        return pltpu.make_async_remote_copy(
            src_ref=src, dst_ref=dst, send_sem=ssem, recv_sem=rsem, device_id=dev(*peer), device_id_type=MESH
        )

    def start(*args):
        one = copy(*args)
        one.start()
        sends.append(one)
        return one

    def arrive(copies):
        for one in copies:
            one.wait_recv()

    near = {}
    for dy in (1, 3):
        for h in (0, 1) if dy == 1 else (1, 0):
            ref = cg.at[y, h]
            near[dy, h] = start(ref, ref, s_cell.at[dy, h], r_cell.at[dy, h], (0, dy, 0, 0))

    def turn(p):
        return jnp.where((p & 1) == 1, (p + 1) // 2, 8 - p // 2)

    def slot_of(p, other):
        return ((z + 8 - turn(p)) & 7) * 2 + (1 - c if other else c)

    def ring_copy(p):
        ref = sg.at[s]
        return copy(ref, ref, s_spot.at[p], r_spot.at[p], (0, 0, turn(p), 0))

    def hand_on(p):
        ref = sg.at[slot_of(p, False)]
        return copy(ref, ref, s_core.at[p], r_core.at[p], sibling)

    own = sg.at[s]
    pair0 = start(own, own, s_core.at[0], r_core.at[0], sibling)
    lax.fori_loop(1, 8, lambda p, carry: (ring_copy(p).start(), carry)[1], 0)
    lab_in = [start(lab.at[y], lab.at[y], s_lab.at[dy], r_lab.at[dy], (0, dy, 0, 0)) for dy in (1, 2, 3)]

    row = lax.broadcasted_iota(jnp.int32, (ROWS, 1), 0)
    centre = jnp.sum(sg[s], axis=1, keepdims=True) * (1.0 / SPT)

    def stack(v, extra, order):
        hi = v.astype(BF16)
        lo = (v - hi.astype(F32)).astype(BF16)
        first = pad_rows((hi.astype(F32) + extra).astype(BF16), SEC)
        hi, lo = pad_rows(hi, SEC), pad_rows(lo, SEC)
        return jnp.concatenate([first] + [(hi, lo)[k] for k in order], axis=0)

    def prep_cells(yy, h):
        lanes = pl.ds(pl.multiple_of(yy * BLK + h * 256, 256), 256)
        v = pad_rows(cg[yy, h] - centre, ROWS)
        pot[0:1, lanes] = jnp.sum(v * v, axis=0, keepdims=True) * SCALE
        extra = jnp.where((row >= PC) & (row < PC + 3), 1.0, 0.0) + jnp.zeros((ROWS, 256), F32)
        ab[:, lanes] = stack(v * (2.0 * SCALE), extra, (0, 1, 1))

    def prep_spots(slot):
        v = pad_rows(sg[slot] - centre, ROWS)
        norm = jnp.sum(v * v, axis=0, keepdims=True) * (-SCALE)
        n1, n2, n3 = pieces3(norm)
        extra = jnp.where(row == PC, n1, 0.0) + jnp.where(row == PC + 1, n2, 0.0) + jnp.where(row == PC + 2, n3, 0.0)
        extra = extra + jnp.where((row >= PC + 3) & (row < PC + 6), 1.0, 0.0)
        block = stack(v, extra, (1, 0, 1))
        bb[:, pl.ds(pl.multiple_of(slot * SPT, SPT), SPT)] = block
        bt[pl.ds(pl.multiple_of(slot * SPT, SPT), SPT), :] = block.T

    def update(slot, yy):
        lanes = pl.ds(pl.multiple_of(yy * BLK, BLK), BLK)
        left = bt[pl.ds(pl.multiple_of(slot * SPT, SPT), SPT), :]
        t = jnp.dot(left, ab[:, lanes], preferred_element_type=F32).reshape(SPT // 8, 8, BLK)
        old = run[0:8, lanes]
        top = jnp.maximum(old, jnp.max(t, axis=0))
        run[8:16, lanes] = run[8:16, lanes] * jnp.exp2(old - top) + jnp.sum(jnp.exp2(t - top[None]), axis=0)
        run[0:8, lanes] = top

    def stream(slots, offsets, fresh=True):
        if fresh:
            for slot in slots:
                prep_spots(slot)
        for slot in slots:
            for dy in offsets:
                update(slot, (y + dy) & 3)

    def got(p):
        ring_copy(p).wait_recv()
        hand_on(p).start()

    prep_cells(y, 0)
    prep_cells(y, 1)
    stream([s], (0,))
    pair0.wait_recv()
    stream([z * 2 + 1 - c], (0,))
    below, above = (y + 3) & 3, (y + 1) & 3
    near[1, 0].wait_recv()
    ref = cg.at[below, 0]
    far0 = start(ref, ref, s_half.at[0], r_half.at[0], (0, 1, 0, 0))
    near[3, 1].wait_recv()
    ref = cg.at[above, 1]
    far1 = start(ref, ref, s_half.at[1], r_half.at[1], (0, 3, 0, 0))
    prep_cells(below, 0)
    prep_cells(above, 1)
    near[1, 1].wait_recv()
    prep_cells(below, 1)
    near[3, 0].wait_recv()
    prep_cells(above, 0)

    got(1)
    got(2)
    stream([slot_of(1, False), slot_of(2, False)], (0, 1, 3))
    stream([s, z * 2 + 1 - c], (1, 3), False)

    def four(k, carry):
        got(2 * k + 1)
        got(2 * k + 2)
        hand_on(2 * k - 1).wait_recv()
        hand_on(2 * k).wait_recv()
        stream(
            [slot_of(2 * k - 1, True), slot_of(2 * k, True), slot_of(2 * k + 1, False), slot_of(2 * k + 2, False)],
            (0, 1, 3),
        )
        return carry

    lax.fori_loop(1, 3, four, 0)
    arrive([far0, far1])
    yy = (y + 2) & 3
    prep_cells(yy, 0)
    prep_cells(yy, 1)
    stream([s, z * 2 + 1 - c] + [slot_of(p, False) for p in (1, 2, 3, 4)], (2,), False)
    got(7)
    stream([slot_of(p, True) for p in (1, 2, 3, 4)] + [slot_of(p, False) for p in (5, 6)], (2,), False)
    hand_on(5).wait_recv()
    hand_on(6).wait_recv()
    stream([slot_of(7, False), slot_of(5, True), slot_of(6, True)], (0, 1, 3, 2))
    hand_on(7).wait_recv()
    stream([slot_of(7, True)], (0, 1, 3, 2))
    top = jnp.max(run[0:8, :], axis=0, keepdims=True)
    total = jnp.sum(run[8:16, :] * jnp.exp2(run[0:8, :] - top), axis=0, keepdims=True)
    rb1[xy] = top + jnp.log2(total) - pot[0:1, :]

    def row_exchange(buf, ssem, rsem):
        return [start(buf.at[xy], buf.at[xy], ssem.at[k], rsem.at[k], peer) for k, peer in enumerate(row_peers)]

    moving = row_exchange(rb1, s_row1, r_row1)
    for k in range(TILE // 256):
        at[k * 256 : (k + 1) * 256, :] = ab[:, k * 256 : (k + 1) * 256].T
    for h in (0, 1):
        for r in range(TILE // 256):
            rows = slice(r * 256, (r + 1) * 256)
            e[h, rows, :] = jnp.dot(at[rows, :], bb[:, h * HALF : (h + 1) * HALF], preferred_element_type=F32)
    arrive(lab_in)
    for k in range(4):
        pot[1:2, k * BLK : (k + 1) * BLK] = lab[k] * LOG2E
    arrive(moving)
    cell1 = pot[1:2, :] - lse(rb1[...], 0)[0]
    pot[2:3, :] = cell1
    f1, f2, f3 = pieces3(cell1 - pot[0:1, :])
    urow[0:1, :] = f1
    urow[1:2, :] = f2
    urow[2:3, :] = f3
    urow[3:8, :] = jnp.zeros((5, TILE), F32)
    sub = lax.broadcasted_iota(jnp.int32, (8, 128), 0)
    ones = jnp.where(sub < 3, 1.0, 0.0).astype(BF16)

    def to_column():
        return lax.dot_general(
            urow[...].astype(BF16), ones, (((0,), (0,)), ((), ())), preferred_element_type=F32
        )

    ucol[...] = to_column()

    def half_lanes(h):
        return pl.ds(pl.multiple_of(h * HALF, HALF), HALF)

    def col_pass(h):
        def step(r, carry):
            for q in range(2):
                at_r = r * 2 + q
                rows = pl.ds(pl.multiple_of(at_r * RB, RB), RB)
                f = ucol[rows, :]
                for k in range(HALF // 128):
                    lanes = slice(k * 128, (k + 1) * 128)
                    v = (e[h, rows, lanes] + f).reshape(RB // 8, 8, 128)
                    top = jnp.max(v, axis=0)
                    w = jnp.exp2(v - top[None])
                    e[h, rows, lanes] = w.reshape(RB, 128)
                    tops[h, at_r, :, lanes] = top
                    sums[at_r, :, lanes] = jnp.sum(w, axis=0)
            return carry

        lax.fori_loop(0, TILE // 256, step, 0)
        part = tops[h].reshape(TILE // RB * 8, HALF)
        top = jnp.max(part, axis=0, keepdims=True)
        total = jnp.sum(sums[...].reshape(TILE // RB * 8, HALF) * jnp.exp2(part - top), axis=0, keepdims=True)
        return top + jnp.log2(total)

    def ring_exchange(buf, ssem, rsem):
        return [start(buf.at[z], buf.at[z], ssem.at[k], rsem.at[k], peer) for k, peer in enumerate(ring_peers)]

    cs1[...] = col_pass(1 - c)
    half = start(cs1, cr1, s_pair.at[0], r_pair.at[0], sibling)
    mine = col_pass(c)
    half.wait_recv()
    cz1[z] = lse(jnp.concatenate([mine, cr1[...]], axis=0), 0)
    arrive(ring_exchange(cz1, s_col1, r_col1))
    gh1[c] = lbb[:, half_lanes(c)] * LOG2E - lse(cz1[...], 0)[0]
    back = start(gh1.at[c], gh1.at[c], s_pair.at[1], r_pair.at[1], sibling)

    def scales(h):
        qrow[h] = jnp.exp2(tops[h] + gh1[h])

    def row_sums(h, last):
        def step(r, carry):
            q = [qrow[h, r, :, j * 128 : (j + 1) * 128] for j in range(HALF // 128)]
            block = pl.ds(pl.multiple_of(r * RB, RB), RB)
            before = ucol[block, :] if last else None
            out = []
            for g in range(RB // 8):
                rows = pl.ds(pl.multiple_of(r * RB + g * 8, 8), 8)
                t = [e[h, rows, j * 128 : (j + 1) * 128] * q[j] for j in range(HALF // 128)]
                while len(t) > 1:
                    t = [t[j] + t[j + 1] for j in range(0, len(t), 2)]
                out.append(t[0])
            out = jnp.concatenate(out, axis=0)
            ucol[block, :] = before + out if last else out
            return carry

        lax.fori_loop(0, TILE // RB, step, 0)

    def to_row():
        for k in range(TILE // 128):
            rows = slice(k * 128, (k + 1) * 128)
            rb2[xy, :, rows] = jnp.sum(ucol[rows, :].T, axis=0, keepdims=True)

    scales(c)
    row_sums(c, False)
    back.wait_recv()
    scales(1 - c)
    row_sums(1 - c, True)
    to_row()
    arrive(row_exchange(rb2, s_row2, r_row2))
    ratio = jnp.exp2(pot[1:2, :]) / jnp.sum(rb2[...], axis=0)
    u1, u2, u3 = pieces3(ratio)
    urow[0:1, :] = u1
    urow[1:2, :] = u2
    urow[2:3, :] = u3
    ucol[...] = to_column()

    def col_sums(h):
        def step(r, t):
            out = [jnp.zeros((8, 128), F32) for k in t]
            for g in range(RB // 8):
                rows = pl.ds(pl.multiple_of(r * RB + g * 8, 8), 8)
                scale = ucol[rows, :]
                for k in range(HALF // 128):
                    out[k] = out[k] + e[h, rows, k * 128 : (k + 1) * 128] * scale
            return tuple(t[k] + out[k] * qrow[h, r, :, k * 128 : (k + 1) * 128] for k in range(HALF // 128))

        parts = lax.fori_loop(0, TILE // RB, step, tuple(jnp.zeros((8, 128), F32) for k in range(HALF // 128)))
        return jnp.sum(jnp.concatenate(parts, axis=1), axis=0, keepdims=True)

    cs2[...] = col_sums(1 - c)
    half = start(cs2, cr2, s_pair.at[2], r_pair.at[2], sibling)
    mine = col_sums(c)
    half.wait_recv()
    cz2[z] = mine + cr2[...]
    moving = ring_exchange(cz2, s_col2, r_col2)
    fo[...] = (pot[2:3, :] + jnp.log2(ratio)) * UNSCALE
    out_f = pltpu.make_async_copy(fo.at[:, pl.ds(pl.multiple_of(y * BLK, BLK), BLK)], outf_ref, l_out.at[0])
    out_f.start()

    def halve(r, carry):
        rows = pl.ds(pl.multiple_of(r * RB, RB), RB)
        for h in (0, 1):
            for j in range(HALF // 256):
                lanes = slice(j * 256, (j + 1) * 256)
                w = (e[h, rows, lanes].reshape(RB // 8, 8, 256) * qrow[h, r, :, lanes][None]).reshape(RB, 256)
                hi = w.astype(BF16)
                eh[h, rows, lanes] = hi
                el[h, rows, lanes] = (w - hi.astype(F32)).astype(BF16)
        return carry

    lax.fori_loop(0, TILE // RB, halve, 0)
    arrive(moving)
    gh2[c] = jnp.exp2(lbb[:, half_lanes(c)] * LOG2E) / jnp.sum(cz2[...], axis=0)
    back = start(gh2.at[c], gh2.at[c], s_pair.at[3], r_pair.at[3], sibling)

    def weigh(h):
        for k in range(8):
            lanes = slice(k * SPT, (k + 1) * SPT)
            v = jnp.where(row == PC, 1.0, pad_rows(sg[h * 8 + k], ROWS)) * gh2[h, :, lanes]
            hi = v.astype(BF16)
            lo = (v - hi.astype(F32)).astype(BF16)
            ptb[h, lanes, :] = jnp.concatenate([pad_rows(hi, SEC), pad_rows(lo, SEC)], axis=0).T

    def product(dy, h):
        rows = pl.ds(pl.multiple_of(((y + dy) & 3) * BLK, BLK), BLK)
        part = jnp.dot(eh[h, rows, :], ptb[h], preferred_element_type=F32)
        return part + jnp.dot(el[h, rows, :], ptb[h], preferred_element_type=F32)

    along_x, along_y, g_in = {}, [], []

    def send_x(dy, part):
        part = part.T
        part = (part[0:ROWS] + part[SEC : SEC + ROWS])[0 : PC + 1]
        for k in range(4):
            stage[dy * 4 + k] = part[:, k * SPT : (k + 1) * SPT]
        along_x[dy] = []
        for dx in (2, 1, 3):
            k = dy * 4 + dx
            src, dst = stage.at[dy * 4 + ((x + dx) & 3)], rs.at[k]
            along_x[dy].append(start(src, dst, s_rs.at[k], r_rs.at[k], (dx, 0, 0, 0)))

    def send_y(dy):
        arrive(along_x[dy])
        k = dy * 4
        xsum[dy] = (stage[k + x] + rs[k + 1]) + (rs[k + 2] + rs[k + 3])
        if dy:
            along_y.append(start(xsum.at[dy], rs.at[k], s_rs.at[k], r_rs.at[k], (0, dy, 0, 0)))

    weigh(c)
    first = product(2, c)
    back.wait_recv()
    weigh(1 - c)
    first = first + product(2, 1 - c)
    second = product(1, c) + product(1, 1 - c)
    send_x(2, first)
    for h in (0, 1):
        gbuf[y, :, h * HALF : (h + 1) * HALF] = (gh1[h] + jnp.log2(gh2[h])) * UNSCALE
    third = product(3, c) + product(3, 1 - c)
    send_x(1, second)
    send_x(3, third)
    fourth = product(0, c) + product(0, 1 - c)
    send_x(0, fourth)
    for dy in (2, 1, 3):
        send_y(dy)
    for dy in (2, 1, 3):
        g_in.append(start(gbuf.at[y], gbuf.at[y], s_g.at[dy], r_g.at[dy], (0, dy, 0, 0)))
    send_y(0)
    arrive(along_y)
    whole = (xsum[0] + rs[4]) + (rs[8] + rs[12])
    ag[x] = whole[0:PC] / whole[PC : PC + 1, :]
    mine = ag.at[x]
    ag_in = [start(mine, mine, s_ag.at[dx], r_ag.at[dx], (dx, 0, 0, 0)) for dx in (2, 1, 3)]
    arrive(g_in)
    outs = [
        pltpu.make_async_copy(gbuf.at[k], outg_ref.at[:, pl.ds(k * TILE, TILE)], l_out.at[1 + k]) for k in range(4)
    ]
    for one in outs:
        one.start()

    def put(k, q):
        lanes = pl.ds(pl.multiple_of(k * SPT, SPT), SPT)
        outs.append(pltpu.make_async_copy(ag.at[k], outb_ref.at[:, lanes], l_out.at[5 + q]))
        outs[-1].start()

    put(x, 0)
    for dx, one in reversed(list(zip((2, 1, 3), ag_in))):
        one.wait_recv()
        put((x - dx) & 3, dx)
    for one in sends:
        one.wait_send()

    def drain(p, carry):
        ring_copy(p).wait_send()
        hand_on(p).wait_send()
        return carry

    lax.fori_loop(1, 8, drain, 0)
    for one in [out_f] + outs:
        one.wait()


def settle(f_ref, g_ref, b_ref, outf_ref, outg_ref, outb_ref):
    outf_ref[...] = f_ref[...]
    outg_ref[...] = g_ref[...]
    outb_ref[...] = b_ref[...]


def on_device(cells_pca, spots_pca, log_a, log_b):
    dma = pltpu.SemaphoreType.DMA
    hbm = pl.BlockSpec(memory_space=pl.ANY)
    vmem = pl.BlockSpec(memory_space=pltpu.VMEM)
    shapes = (
        jax.ShapeDtypeStruct((1, BLK), F32),
        jax.ShapeDtypeStruct((1, 4 * TILE), F32),
        jax.ShapeDtypeStruct((PC, BLK), F32),
    )
    pairs = ((4, 2), (2,), (4,), (8,), (8,), (15,), (15,), (4,), (7,), (7,), (4,), (16,), (4,))
    out = pl.pallas_call(
        kernel,
        out_shape=shapes,
        in_specs=[hbm] * 4,
        out_specs=(hbm,) * 3,
        scratch_shapes=[
            pltpu.VMEM((4, 2, PC, 256), F32),
            pltpu.VMEM((4, 1, BLK), F32),
            pltpu.VMEM((1, TILE), F32),
            pltpu.VMEM((16, PC, SPT), F32),
            pltpu.VMEM((4 * SEC, TILE), BF16),
            pltpu.VMEM((4 * SEC, TILE), BF16),
            pltpu.VMEM((TILE, 4 * SEC), BF16),
            pltpu.VMEM((2, TILE, HALF), F32),
            pltpu.VMEM((16, TILE), F32),
            pltpu.VMEM((TILE, 128), F32),
            pltpu.VMEM((8, TILE), F32),
            pltpu.VMEM((16, 1, TILE), F32),
            pltpu.VMEM((16, 1, TILE), F32),
            pltpu.VMEM((1, HALF), F32),
            pltpu.VMEM((1, HALF), F32),
            pltpu.VMEM((8, 1, HALF), F32),
            pltpu.VMEM((2, 1, HALF), F32),
            pltpu.VMEM((1, HALF), F32),
            pltpu.VMEM((1, HALF), F32),
            pltpu.VMEM((8, 1, HALF), F32),
            pltpu.VMEM((2, 1, HALF), F32),
            pltpu.VMEM((4, 1, TILE), F32),
            pltpu.VMEM((16, PC + 1, SPT), F32),
            pltpu.VMEM((16, PC + 1, SPT), F32),
            pltpu.VMEM((4, PC, SPT), F32),
            pltpu.VMEM((8, TILE), F32),
            pltpu.VMEM((1, TILE), F32),
            pltpu.VMEM((2, TILE // RB, 8, HALF), F32),
            pltpu.VMEM((TILE // RB, 8, HALF), F32),
            pltpu.VMEM((2, TILE // RB, 8, HALF), F32),
            pltpu.VMEM((2, HALF, 2 * SEC), BF16),
            pltpu.VMEM((2, TILE, HALF), BF16),
            pltpu.VMEM((2, TILE, HALF), BF16),
            pltpu.VMEM((TILE, 4 * SEC), BF16),
            pltpu.VMEM((4, PC + 1, SPT), F32),
            dma((5,)),
        ]
        + [dma(n) for n in pairs for _ in range(2)]
        + [dma((9,))],
        compiler_params=pltpu.CompilerParams(
            collective_id=0, has_side_effects=True, vmem_limit_bytes=58 * 2**20
        ),
        cost_estimate=pl.CostEstimate(flops=10 * 2**30, bytes_accessed=2**20, transcendentals=2**23),
        name="sinkhorn",
    )(cells_pca, spots_pca, log_a.reshape(1, BLK), log_b.reshape(1, 4 * TILE))
    f, g, bary = pl.pallas_call(
        settle,
        out_shape=shapes,
        in_specs=[vmem] * 3,
        out_specs=(vmem,) * 3,
        name="settle",
    )(*out)
    return f.reshape(BLK), g.reshape(4 * TILE), bary


def solution(mesh):
    placed = (P(None, "cell"), P(None, ("spot", "cell")), P("cell"), P("spot"))
    return jax.shard_map(
        on_device,
        mesh=mesh,
        in_specs=placed,
        out_specs=(P("cell"), P("spot"), P(None, "cell")),
        check_vma=False,
    )
```

```python
import math

import jax
import jax.numpy as jnp
from jax import lax
from jax.experimental import pallas as pl
from jax.experimental.pallas import tpu as pltpu
from jax.sharding import PartitionSpec as P

MESH = pl.DeviceIdType.MESH
F32, BF16 = jnp.float32, jnp.bfloat16

PC = 50
ROWS = 56
SEC = 64
TILE = 2048
BLK = 512
HALF = TILE // 2
SPT = 128
RB = 128
blur = 0.25
LOG2E = math.log2(math.e)
SCALE = LOG2E / blur
UNSCALE = blur / LOG2E


def pieces3(v):
    one = v.astype(BF16).astype(F32)
    rest = v - one
    two = rest.astype(BF16).astype(F32)
    return one, two, (rest - two).astype(BF16).astype(F32)


def pad_rows(v, rows):
    return jnp.concatenate([v, jnp.zeros((rows - v.shape[0], v.shape[1]), v.dtype)], axis=0)


def lse(v, axis):
    top = jnp.max(v, axis=axis, keepdims=True)
    out = top + jnp.log2(jnp.sum(jnp.exp2(v - top), axis=axis, keepdims=True))
    return out


def kernel(
    cells_ref, spots_ref, loga_ref, logb_ref, outf_ref, outg_ref, outb_ref,
    cg, lab, lbb, sg, ab, bb, at, e, run, ucol, urow, rb1, rb2, cs1, cr1, cz1, gh1, cs2, cr2, cz2, gh2, gbuf, stage, rs, ag,
    pot, fo, tops, sums, qrow, ptb, eh, el, bt, xsum,
    l_in, s_cell, r_cell, s_half, r_half, s_lab, r_lab, s_spot, r_spot, s_core, r_core, s_row1, r_row1, s_row2, r_row2,
    s_pair, r_pair, s_col1, r_col1, s_col2, r_col2, s_g, r_g, s_rs, r_rs, s_ag, r_ag, l_out,
):
    b = lax.axis_index("cell")
    x = lax.axis_index("spot")
    s = b & 15
    y, z, c = b // 16, s // 2, b & 1
    xy = x * 4 + y

    def dev(dx, dy, dz, dc):
        px, py, pz, pc = (x + dx) & 3, (y + dy) & 3, (z + dz) & 7, (c + dc) & 1
        return ((py * 8 + pz) * 2 + pc, px)

    row_peers = [(dx, dy, 0, 0) for dx in (2, 1, 3, 0) for dy in (2, 1, 3, 0) if dx or dy]
    ring = (4, 3, 5, 2, 6, 1, 7)
    ring_peers = [(0, 0, dz, 0) for dz in ring]
    sibling = (0, 0, 0, 1)
    peers = row_peers + ring_peers + [sibling]
    barrier = pltpu.get_barrier_semaphore()
    for peer in peers:
        pl.semaphore_signal(barrier, inc=1, device_id=dev(*peer), device_id_type=MESH)

    loads = [
        pltpu.make_async_copy(cells_ref.at[:, pl.ds(0, 256)], cg.at[y, 0], l_in.at[0]),
        pltpu.make_async_copy(cells_ref.at[:, pl.ds(256, 256)], cg.at[y, 1], l_in.at[1]),
        pltpu.make_async_copy(spots_ref, sg.at[s], l_in.at[2]),
        pltpu.make_async_copy(loga_ref, lab.at[y], l_in.at[3]),
        pltpu.make_async_copy(logb_ref.at[:, pl.ds(pl.multiple_of(y * TILE, TILE), TILE)], lbb, l_in.at[4]),
    ]
    for one in loads:
        one.start()
    run[0:8, :] = jnp.full((8, TILE), -jnp.inf, F32)
    run[8:16, :] = jnp.zeros((8, TILE), F32)
    for one in loads:
        one.wait()
    pl.semaphore_wait(barrier, len(peers))

    sends = []

    def copy(src, dst, ssem, rsem, peer):
        return pltpu.make_async_remote_copy(
            src_ref=src, dst_ref=dst, send_sem=ssem, recv_sem=rsem, device_id=dev(*peer), device_id_type=MESH
        )

    def start(*args):
        one = copy(*args)
        one.start()
        sends.append(one)
        return one

    def arrive(copies):
        for one in copies:
            one.wait_recv()

    near = {}
    for dy in (1, 3):
        for h in (0, 1) if dy == 1 else (1, 0):
            ref = cg.at[y, h]
            near[dy, h] = start(ref, ref, s_cell.at[dy, h], r_cell.at[dy, h], (0, dy, 0, 0))

    def turn(p):
        return jnp.where((p & 1) == 1, (p + 1) // 2, 8 - p // 2)

    def slot_of(p, other):
        return ((z + 8 - turn(p)) & 7) * 2 + (1 - c if other else c)

    def ring_copy(p):
        ref = sg.at[s]
        return copy(ref, ref, s_spot.at[p], r_spot.at[p], (0, 0, turn(p), 0))

    def hand_on(p):
        ref = sg.at[slot_of(p, False)]
        return copy(ref, ref, s_core.at[p], r_core.at[p], sibling)

    own = sg.at[s]
    pair0 = start(own, own, s_core.at[0], r_core.at[0], sibling)
    lax.fori_loop(1, 8, lambda p, carry: (ring_copy(p).start(), carry)[1], 0)
    lab_in = [start(lab.at[y], lab.at[y], s_lab.at[dy], r_lab.at[dy], (0, dy, 0, 0)) for dy in (1, 2, 3)]

    row = lax.broadcasted_iota(jnp.int32, (ROWS, 1), 0)
    centre = jnp.sum(sg[s], axis=1, keepdims=True) * (1.0 / SPT)

    def stack(v, extra, order):
        hi = v.astype(BF16)
        lo = (v - hi.astype(F32)).astype(BF16)
        first = pad_rows((hi.astype(F32) + extra).astype(BF16), SEC)
        hi, lo = pad_rows(hi, SEC), pad_rows(lo, SEC)
        return jnp.concatenate([first] + [(hi, lo)[k] for k in order], axis=0)

    def prep_cells(yy, h):
        lanes = pl.ds(pl.multiple_of(yy * BLK + h * 256, 256), 256)
        v = pad_rows(cg[yy, h] - centre, ROWS)
        pot[0:1, lanes] = jnp.sum(v * v, axis=0, keepdims=True) * SCALE
        extra = jnp.where((row >= PC) & (row < PC + 3), 1.0, 0.0) + jnp.zeros((ROWS, 256), F32)
        ab[:, lanes] = stack(v * (2.0 * SCALE), extra, (0, 1, 1))

    def prep_spots(slot):
        v = pad_rows(sg[slot] - centre, ROWS)
        norm = jnp.sum(v * v, axis=0, keepdims=True) * (-SCALE)
        n1, n2, n3 = pieces3(norm)
        extra = jnp.where(row == PC, n1, 0.0) + jnp.where(row == PC + 1, n2, 0.0) + jnp.where(row == PC + 2, n3, 0.0)
        extra = extra + jnp.where((row >= PC + 3) & (row < PC + 6), 1.0, 0.0)
        block = stack(v, extra, (1, 0, 1))
        bb[:, pl.ds(pl.multiple_of(slot * SPT, SPT), SPT)] = block
        bt[pl.ds(pl.multiple_of(slot * SPT, SPT), SPT), :] = block.T

    def update(slot, yy):
        lanes = pl.ds(pl.multiple_of(yy * BLK, BLK), BLK)
        left = bt[pl.ds(pl.multiple_of(slot * SPT, SPT), SPT), :]
        t = jnp.dot(left, ab[:, lanes], preferred_element_type=F32).reshape(SPT // 8, 8, BLK)
        old = run[0:8, lanes]
        top = jnp.maximum(old, jnp.max(t, axis=0))
        run[8:16, lanes] = run[8:16, lanes] * jnp.exp2(old - top) + jnp.sum(jnp.exp2(t - top[None]), axis=0)
        run[0:8, lanes] = top

    def stream(slots, offsets, fresh=True):
        if fresh:
            for slot in slots:
                prep_spots(slot)
        for slot in slots:
            for dy in offsets:
                update(slot, (y + dy) & 3)

    def got(p):
        ring_copy(p).wait_recv()
        hand_on(p).start()

    prep_cells(y, 0)
    prep_cells(y, 1)
    stream([s], (0,))
    pair0.wait_recv()
    stream([z * 2 + 1 - c], (0,))
    below, above = (y + 3) & 3, (y + 1) & 3
    near[1, 0].wait_recv()
    ref = cg.at[below, 0]
    far0 = start(ref, ref, s_half.at[0], r_half.at[0], (0, 1, 0, 0))
    near[3, 1].wait_recv()
    ref = cg.at[above, 1]
    far1 = start(ref, ref, s_half.at[1], r_half.at[1], (0, 3, 0, 0))
    got(1)
    got(2)
    stream([slot_of(1, False), slot_of(2, False)], (0,))
    prep_cells(below, 0)
    prep_cells(above, 1)
    near[1, 1].wait_recv()
    prep_cells(below, 1)
    near[3, 0].wait_recv()
    prep_cells(above, 0)

    stream([s, z * 2 + 1 - c, slot_of(1, False), slot_of(2, False)], (1, 3), False)

    def four(k, carry):
        got(2 * k + 1)
        got(2 * k + 2)
        hand_on(2 * k - 1).wait_recv()
        hand_on(2 * k).wait_recv()
        stream(
            [slot_of(2 * k - 1, True), slot_of(2 * k, True), slot_of(2 * k + 1, False), slot_of(2 * k + 2, False)],
            (0, 1, 3),
        )
        return carry

    lax.fori_loop(1, 3, four, 0)
    arrive([far0, far1])
    yy = (y + 2) & 3
    prep_cells(yy, 0)
    prep_cells(yy, 1)
    stream([s, z * 2 + 1 - c] + [slot_of(p, False) for p in (1, 2, 3, 4)], (2,), False)
    got(7)
    stream([slot_of(p, True) for p in (1, 2, 3, 4)] + [slot_of(p, False) for p in (5, 6)], (2,), False)
    hand_on(5).wait_recv()
    hand_on(6).wait_recv()
    stream([slot_of(7, False), slot_of(5, True), slot_of(6, True)], (0, 1, 3, 2))
    hand_on(7).wait_recv()
    stream([slot_of(7, True)], (0, 1, 3, 2))
    top = jnp.max(run[0:8, :], axis=0, keepdims=True)
    total = jnp.sum(run[8:16, :] * jnp.exp2(run[0:8, :] - top), axis=0, keepdims=True)
    rb1[xy] = top + jnp.log2(total) - pot[0:1, :]

    def row_exchange(buf, ssem, rsem):
        return [start(buf.at[xy], buf.at[xy], ssem.at[k], rsem.at[k], peer) for k, peer in enumerate(row_peers)]

    moving = row_exchange(rb1, s_row1, r_row1)
    for k in range(TILE // 256):
        at[k * 256 : (k + 1) * 256, :] = ab[:, k * 256 : (k + 1) * 256].T
    for h in (0, 1):
        for r in range(TILE // 256):
            rows = slice(r * 256, (r + 1) * 256)
            e[h, rows, :] = jnp.dot(at[rows, :], bb[:, h * HALF : (h + 1) * HALF], preferred_element_type=F32)
    arrive(lab_in)
    for k in range(4):
        pot[1:2, k * BLK : (k + 1) * BLK] = lab[k] * LOG2E
    arrive(moving)
    cell1 = pot[1:2, :] - lse(rb1[...], 0)[0]
    pot[2:3, :] = cell1
    f1, f2, f3 = pieces3(cell1 - pot[0:1, :])
    urow[0:1, :] = f1
    urow[1:2, :] = f2
    urow[2:3, :] = f3
    urow[3:8, :] = jnp.zeros((5, TILE), F32)
    sub = lax.broadcasted_iota(jnp.int32, (8, 128), 0)
    ones = jnp.where(sub < 3, 1.0, 0.0).astype(BF16)

    def to_column():
        return lax.dot_general(
            urow[...].astype(BF16), ones, (((0,), (0,)), ((), ())), preferred_element_type=F32
        )

    ucol[...] = to_column()

    def half_lanes(h):
        return pl.ds(pl.multiple_of(h * HALF, HALF), HALF)

    def col_pass(h):
        def step(r, carry):
            for q in range(2):
                at_r = r * 2 + q
                rows = pl.ds(pl.multiple_of(at_r * RB, RB), RB)
                f = ucol[rows, :]
                for k in range(HALF // 128):
                    lanes = slice(k * 128, (k + 1) * 128)
                    v = (e[h, rows, lanes] + f).reshape(RB // 8, 8, 128)
                    top = jnp.max(v, axis=0)
                    w = jnp.exp2(v - top[None])
                    e[h, rows, lanes] = w.reshape(RB, 128)
                    tops[h, at_r, :, lanes] = top
                    sums[at_r, :, lanes] = jnp.sum(w, axis=0)
            return carry

        lax.fori_loop(0, TILE // 256, step, 0)
        part = tops[h].reshape(TILE // RB * 8, HALF)
        top = jnp.max(part, axis=0, keepdims=True)
        total = jnp.sum(sums[...].reshape(TILE // RB * 8, HALF) * jnp.exp2(part - top), axis=0, keepdims=True)
        return top + jnp.log2(total)

    def ring_exchange(buf, ssem, rsem):
        return [start(buf.at[z], buf.at[z], ssem.at[k], rsem.at[k], peer) for k, peer in enumerate(ring_peers)]

    cs1[...] = col_pass(1 - c)
    half = start(cs1, cr1, s_pair.at[0], r_pair.at[0], sibling)
    mine = col_pass(c)
    half.wait_recv()
    cz1[z] = lse(jnp.concatenate([mine, cr1[...]], axis=0), 0)
    arrive(ring_exchange(cz1, s_col1, r_col1))
    gh1[c] = lbb[:, half_lanes(c)] * LOG2E - lse(cz1[...], 0)[0]
    back = start(gh1.at[c], gh1.at[c], s_pair.at[1], r_pair.at[1], sibling)

    def scales(h):
        qrow[h] = jnp.exp2(tops[h] + gh1[h])

    def row_sums(h, last):
        def step(r, carry):
            q = [qrow[h, r, :, j * 128 : (j + 1) * 128] for j in range(HALF // 128)]
            block = pl.ds(pl.multiple_of(r * RB, RB), RB)
            before = ucol[block, :] if last else None
            out = []
            for g in range(RB // 8):
                rows = pl.ds(pl.multiple_of(r * RB + g * 8, 8), 8)
                t = [e[h, rows, j * 128 : (j + 1) * 128] * q[j] for j in range(HALF // 128)]
                while len(t) > 1:
                    t = [t[j] + t[j + 1] for j in range(0, len(t), 2)]
                out.append(t[0])
            out = jnp.concatenate(out, axis=0)
            ucol[block, :] = before + out if last else out
            return carry

        lax.fori_loop(0, TILE // RB, step, 0)

    def to_row():
        for k in range(TILE // 128):
            rows = slice(k * 128, (k + 1) * 128)
            rb2[xy, :, rows] = jnp.sum(ucol[rows, :].T, axis=0, keepdims=True)

    scales(c)
    row_sums(c, False)
    back.wait_recv()
    scales(1 - c)
    row_sums(1 - c, True)
    to_row()
    arrive(row_exchange(rb2, s_row2, r_row2))
    ratio = jnp.exp2(pot[1:2, :]) / jnp.sum(rb2[...], axis=0)
    u1, u2, u3 = pieces3(ratio)
    urow[0:1, :] = u1
    urow[1:2, :] = u2
    urow[2:3, :] = u3
    ucol[...] = to_column()

    def col_sums(h):
        def step(r, t):
            out = [jnp.zeros((8, 128), F32) for k in t]
            for g in range(RB // 8):
                rows = pl.ds(pl.multiple_of(r * RB + g * 8, 8), 8)
                scale = ucol[rows, :]
                for k in range(HALF // 128):
                    out[k] = out[k] + e[h, rows, k * 128 : (k + 1) * 128] * scale
            return tuple(t[k] + out[k] * qrow[h, r, :, k * 128 : (k + 1) * 128] for k in range(HALF // 128))

        parts = lax.fori_loop(0, TILE // RB, step, tuple(jnp.zeros((8, 128), F32) for k in range(HALF // 128)))
        return jnp.sum(jnp.concatenate(parts, axis=1), axis=0, keepdims=True)

    cs2[...] = col_sums(1 - c)
    half = start(cs2, cr2, s_pair.at[2], r_pair.at[2], sibling)
    mine = col_sums(c)
    half.wait_recv()
    cz2[z] = mine + cr2[...]
    moving = ring_exchange(cz2, s_col2, r_col2)
    fo[...] = (pot[2:3, :] + jnp.log2(ratio)) * UNSCALE
    out_f = pltpu.make_async_copy(fo.at[:, pl.ds(pl.multiple_of(y * BLK, BLK), BLK)], outf_ref, l_out.at[0])
    out_f.start()

    def halve(r, carry):
        rows = pl.ds(pl.multiple_of(r * RB, RB), RB)
        for h in (0, 1):
            for j in range(HALF // 256):
                lanes = slice(j * 256, (j + 1) * 256)
                w = (e[h, rows, lanes].reshape(RB // 8, 8, 256) * qrow[h, r, :, lanes][None]).reshape(RB, 256)
                hi = w.astype(BF16)
                eh[h, rows, lanes] = hi
                el[h, rows, lanes] = (w - hi.astype(F32)).astype(BF16)
        return carry

    lax.fori_loop(0, TILE // RB, halve, 0)
    arrive(moving)
    gh2[c] = jnp.exp2(lbb[:, half_lanes(c)] * LOG2E) / jnp.sum(cz2[...], axis=0)
    back = start(gh2.at[c], gh2.at[c], s_pair.at[3], r_pair.at[3], sibling)

    def weigh(h):
        for k in range(8):
            lanes = slice(k * SPT, (k + 1) * SPT)
            v = jnp.where(row == PC, 1.0, pad_rows(sg[h * 8 + k], ROWS)) * gh2[h, :, lanes]
            hi = v.astype(BF16)
            lo = (v - hi.astype(F32)).astype(BF16)
            ptb[h, lanes, :] = jnp.concatenate([pad_rows(hi, SEC), pad_rows(lo, SEC)], axis=0).T

    def product(dy, h):
        rows = pl.ds(pl.multiple_of(((y + dy) & 3) * BLK, BLK), BLK)
        part = jnp.dot(eh[h, rows, :], ptb[h], preferred_element_type=F32)
        return part + jnp.dot(el[h, rows, :], ptb[h], preferred_element_type=F32)

    along_x, along_y, g_in = {}, [], []

    def send_x(dy, part):
        part = part.T
        part = (part[0:ROWS] + part[SEC : SEC + ROWS])[0 : PC + 1]
        for k in range(4):
            stage[dy * 4 + k] = part[:, k * SPT : (k + 1) * SPT]
        along_x[dy] = []
        for dx in (2, 1, 3):
            k = dy * 4 + dx
            src, dst = stage.at[dy * 4 + ((x + dx) & 3)], rs.at[k]
            along_x[dy].append(start(src, dst, s_rs.at[k], r_rs.at[k], (dx, 0, 0, 0)))

    def send_y(dy):
        arrive(along_x[dy])
        k = dy * 4
        xsum[dy] = (stage[k + x] + rs[k + 1]) + (rs[k + 2] + rs[k + 3])
        if dy:
            along_y.append(start(xsum.at[dy], rs.at[k], s_rs.at[k], r_rs.at[k], (0, dy, 0, 0)))

    weigh(c)
    first = product(2, c)
    back.wait_recv()
    weigh(1 - c)
    first = first + product(2, 1 - c)
    second = product(1, c) + product(1, 1 - c)
    send_x(2, first)
    for h in (0, 1):
        gbuf[y, :, h * HALF : (h + 1) * HALF] = (gh1[h] + jnp.log2(gh2[h])) * UNSCALE
    third = product(3, c) + product(3, 1 - c)
    send_x(1, second)
    send_x(3, third)
    fourth = product(0, c) + product(0, 1 - c)
    send_x(0, fourth)
    for dy in (2, 1, 3):
        send_y(dy)
    for dy in (2, 1, 3):
        g_in.append(start(gbuf.at[y], gbuf.at[y], s_g.at[dy], r_g.at[dy], (0, dy, 0, 0)))
    send_y(0)
    arrive(along_y)
    whole = (xsum[0] + rs[4]) + (rs[8] + rs[12])
    ag[x] = whole[0:PC] / whole[PC : PC + 1, :]
    mine = ag.at[x]
    ag_in = [start(mine, mine, s_ag.at[dx], r_ag.at[dx], (dx, 0, 0, 0)) for dx in (2, 1, 3)]
    arrive(g_in)
    outs = [
        pltpu.make_async_copy(gbuf.at[k], outg_ref.at[:, pl.ds(k * TILE, TILE)], l_out.at[1 + k]) for k in range(4)
    ]
    for one in outs:
        one.start()

    def put(k, q):
        lanes = pl.ds(pl.multiple_of(k * SPT, SPT), SPT)
        outs.append(pltpu.make_async_copy(ag.at[k], outb_ref.at[:, lanes], l_out.at[5 + q]))
        outs[-1].start()

    put(x, 0)
    for dx, one in reversed(list(zip((2, 1, 3), ag_in))):
        one.wait_recv()
        put((x - dx) & 3, dx)
    for one in sends:
        one.wait_send()

    def drain(p, carry):
        ring_copy(p).wait_send()
        hand_on(p).wait_send()
        return carry

    lax.fori_loop(1, 8, drain, 0)
    for one in [out_f] + outs:
        one.wait()


def settle(f_ref, g_ref, b_ref, outf_ref, outg_ref, outb_ref):
    outf_ref[...] = f_ref[...]
    outg_ref[...] = g_ref[...]
    outb_ref[...] = b_ref[...]


def on_device(cells_pca, spots_pca, log_a, log_b):
    dma = pltpu.SemaphoreType.DMA
    hbm = pl.BlockSpec(memory_space=pl.ANY)
    vmem = pl.BlockSpec(memory_space=pltpu.VMEM)
    shapes = (
        jax.ShapeDtypeStruct((1, BLK), F32),
        jax.ShapeDtypeStruct((1, 4 * TILE), F32),
        jax.ShapeDtypeStruct((PC, BLK), F32),
    )
    pairs = ((4, 2), (2,), (4,), (8,), (8,), (15,), (15,), (4,), (7,), (7,), (4,), (16,), (4,))
    out = pl.pallas_call(
        kernel,
        out_shape=shapes,
        in_specs=[hbm] * 4,
        out_specs=(hbm,) * 3,
        scratch_shapes=[
            pltpu.VMEM((4, 2, PC, 256), F32),
            pltpu.VMEM((4, 1, BLK), F32),
            pltpu.VMEM((1, TILE), F32),
            pltpu.VMEM((16, PC, SPT), F32),
            pltpu.VMEM((4 * SEC, TILE), BF16),
            pltpu.VMEM((4 * SEC, TILE), BF16),
            pltpu.VMEM((TILE, 4 * SEC), BF16),
            pltpu.VMEM((2, TILE, HALF), F32),
            pltpu.VMEM((16, TILE), F32),
            pltpu.VMEM((TILE, 128), F32),
            pltpu.VMEM((8, TILE), F32),
            pltpu.VMEM((16, 1, TILE), F32),
            pltpu.VMEM((16, 1, TILE), F32),
            pltpu.VMEM((1, HALF), F32),
            pltpu.VMEM((1, HALF), F32),
            pltpu.VMEM((8, 1, HALF), F32),
            pltpu.VMEM((2, 1, HALF), F32),
            pltpu.VMEM((1, HALF), F32),
            pltpu.VMEM((1, HALF), F32),
            pltpu.VMEM((8, 1, HALF), F32),
            pltpu.VMEM((2, 1, HALF), F32),
            pltpu.VMEM((4, 1, TILE), F32),
            pltpu.VMEM((16, PC + 1, SPT), F32),
            pltpu.VMEM((16, PC + 1, SPT), F32),
            pltpu.VMEM((4, PC, SPT), F32),
            pltpu.VMEM((8, TILE), F32),
            pltpu.VMEM((1, TILE), F32),
            pltpu.VMEM((2, TILE // RB, 8, HALF), F32),
            pltpu.VMEM((TILE // RB, 8, HALF), F32),
            pltpu.VMEM((2, TILE // RB, 8, HALF), F32),
            pltpu.VMEM((2, HALF, 2 * SEC), BF16),
            pltpu.VMEM((2, TILE, HALF), BF16),
            pltpu.VMEM((2, TILE, HALF), BF16),
            pltpu.VMEM((TILE, 4 * SEC), BF16),
            pltpu.VMEM((4, PC + 1, SPT), F32),
            dma((5,)),
        ]
        + [dma(n) for n in pairs for _ in range(2)]
        + [dma((9,))],
        compiler_params=pltpu.CompilerParams(
            collective_id=0, has_side_effects=True, vmem_limit_bytes=58 * 2**20
        ),
        cost_estimate=pl.CostEstimate(flops=10 * 2**30, bytes_accessed=2**20, transcendentals=2**23),
        name="sinkhorn",
    )(cells_pca, spots_pca, log_a.reshape(1, BLK), log_b.reshape(1, 4 * TILE))
    f, g, bary = pl.pallas_call(
        settle,
        out_shape=shapes,
        in_specs=[vmem] * 3,
        out_specs=(vmem,) * 3,
        name="settle",
    )(*out)
    return f.reshape(BLK), g.reshape(4 * TILE), bary


def solution(mesh):
    placed = (P(None, "cell"), P(None, ("spot", "cell")), P("cell"), P("spot"))
    return jax.shard_map(
        on_device,
        mesh=mesh,
        in_specs=placed,
        out_specs=(P("cell"), P("spot"), P(None, "cell")),
        check_vma=False,
    )
```

```python
import math

import jax
import jax.numpy as jnp
from jax import lax
from jax.experimental import pallas as pl
from jax.experimental.pallas import tpu as pltpu
from jax.sharding import PartitionSpec as P

MESH = pl.DeviceIdType.MESH
F32, BF16 = jnp.float32, jnp.bfloat16

PC = 50
ROWS = 56
SEC = 64
TILE = 2048
BLK = 512
HALF = TILE // 2
SPT = 128
RB = 128
blur = 0.25
LOG2E = math.log2(math.e)
SCALE = LOG2E / blur
UNSCALE = blur / LOG2E


def pieces3(v):
    one = v.astype(BF16).astype(F32)
    rest = v - one
    two = rest.astype(BF16).astype(F32)
    return one, two, (rest - two).astype(BF16).astype(F32)


def pad_rows(v, rows):
    return jnp.concatenate([v, jnp.zeros((rows - v.shape[0], v.shape[1]), v.dtype)], axis=0)


def lse(v, axis):
    top = jnp.max(v, axis=axis, keepdims=True)
    out = top + jnp.log2(jnp.sum(jnp.exp2(v - top), axis=axis, keepdims=True))
    return out


def kernel(
    cells_ref, spots_ref, loga_ref, logb_ref, outf_ref, outg_ref, outb_ref,
    cg, lab, lbb, sg, ab, bb, at, e, run, ucol, urow, rb1, rb2, cs1, cr1, cz1, gh1, cs2, cr2, cz2, gh2, gbuf, stage, rs, ag,
    pot, fo, tops, sums, qrow, ptb, eh, el, bt, xsum,
    l_in, s_cell, r_cell, s_half, r_half, s_lab, r_lab, s_spot, r_spot, s_core, r_core, s_row1, r_row1, s_row2, r_row2,
    s_pair, r_pair, s_col1, r_col1, s_col2, r_col2, s_g, r_g, s_rs, r_rs, s_ag, r_ag, l_out,
):
    b = lax.axis_index("cell")
    x = lax.axis_index("spot")
    s = b & 15
    y, z, c = b // 16, s // 2, b & 1
    xy = x * 4 + y

    def dev(dx, dy, dz, dc):
        px, py, pz, pc = (x + dx) & 3, (y + dy) & 3, (z + dz) & 7, (c + dc) & 1
        return ((py * 8 + pz) * 2 + pc, px)

    row_peers = [(dx, dy, 0, 0) for dx in (2, 1, 3, 0) for dy in (2, 1, 3, 0) if dx or dy]
    ring = (4, 3, 5, 2, 6, 1, 7)
    ring_peers = [(0, 0, dz, 0) for dz in ring]
    sibling = (0, 0, 0, 1)
    peers = row_peers + ring_peers + [sibling]
    barrier = pltpu.get_barrier_semaphore()
    for peer in peers:
        pl.semaphore_signal(barrier, inc=1, device_id=dev(*peer), device_id_type=MESH)

    loads = [
        pltpu.make_async_copy(cells_ref.at[:, pl.ds(0, 256)], cg.at[y, 0], l_in.at[0]),
        pltpu.make_async_copy(cells_ref.at[:, pl.ds(256, 256)], cg.at[y, 1], l_in.at[1]),
        pltpu.make_async_copy(spots_ref, sg.at[s], l_in.at[2]),
        pltpu.make_async_copy(loga_ref, lab.at[y], l_in.at[3]),
        pltpu.make_async_copy(logb_ref.at[:, pl.ds(pl.multiple_of(y * TILE, TILE), TILE)], lbb, l_in.at[4]),
    ]
    for one in loads:
        one.start()
    run[0:8, :] = jnp.full((8, TILE), -jnp.inf, F32)
    run[8:16, :] = jnp.zeros((8, TILE), F32)
    for one in loads:
        one.wait()
    pl.semaphore_wait(barrier, len(peers))

    sends = []

    def copy(src, dst, ssem, rsem, peer):
        return pltpu.make_async_remote_copy(
            src_ref=src, dst_ref=dst, send_sem=ssem, recv_sem=rsem, device_id=dev(*peer), device_id_type=MESH
        )

    def start(*args):
        one = copy(*args)
        one.start()
        sends.append(one)
        return one

    def settled(count):
        for one in sends[:count]:
            one.wait_send()
        del sends[:count]

    def arrive(copies):
        for one in copies:
            one.wait_recv()

    near = {}
    for dy in (1, 3):
        for h in (0, 1) if dy == 1 else (1, 0):
            ref = cg.at[y, h]
            near[dy, h] = start(ref, ref, s_cell.at[dy, h], r_cell.at[dy, h], (0, dy, 0, 0))

    def turn(p):
        return jnp.where((p & 1) == 1, (p + 1) // 2, 8 - p // 2)

    def slot_of(p, other):
        return ((z + 8 - turn(p)) & 7) * 2 + (1 - c if other else c)

    def ring_copy(p):
        ref = sg.at[s]
        return copy(ref, ref, s_spot.at[p], r_spot.at[p], (0, 0, turn(p), 0))

    def hand_on(p):
        ref = sg.at[slot_of(p, False)]
        return copy(ref, ref, s_core.at[p], r_core.at[p], sibling)

    own = sg.at[s]
    pair0 = start(own, own, s_core.at[0], r_core.at[0], sibling)
    lax.fori_loop(1, 8, lambda p, carry: (ring_copy(p).start(), carry)[1], 0)
    lab_in = [start(lab.at[y], lab.at[y], s_lab.at[dy], r_lab.at[dy], (0, dy, 0, 0)) for dy in (1, 2, 3)]

    row = lax.broadcasted_iota(jnp.int32, (ROWS, 1), 0)
    centre = jnp.sum(sg[s], axis=1, keepdims=True) * (1.0 / SPT)

    def stack(v, extra, order):
        hi = v.astype(BF16)
        lo = (v - hi.astype(F32)).astype(BF16)
        first = pad_rows((hi.astype(F32) + extra).astype(BF16), SEC)
        hi, lo = pad_rows(hi, SEC), pad_rows(lo, SEC)
        return jnp.concatenate([first] + [(hi, lo)[k] for k in order], axis=0)

    def prep_cells(yy, h):
        lanes = pl.ds(pl.multiple_of(yy * BLK + h * 256, 256), 256)
        v = pad_rows(cg[yy, h] - centre, ROWS)
        pot[0:1, lanes] = jnp.sum(v * v, axis=0, keepdims=True) * SCALE
        extra = jnp.where((row >= PC) & (row < PC + 3), 1.0, 0.0) + jnp.zeros((ROWS, 256), F32)
        ab[:, lanes] = stack(v * (2.0 * SCALE), extra, (0, 1, 1))

    def prep_spots(slot):
        v = pad_rows(sg[slot] - centre, ROWS)
        norm = jnp.sum(v * v, axis=0, keepdims=True) * (-SCALE)
        n1, n2, n3 = pieces3(norm)
        extra = jnp.where(row == PC, n1, 0.0) + jnp.where(row == PC + 1, n2, 0.0) + jnp.where(row == PC + 2, n3, 0.0)
        extra = extra + jnp.where((row >= PC + 3) & (row < PC + 6), 1.0, 0.0)
        block = stack(v, extra, (1, 0, 1))
        bb[:, pl.ds(pl.multiple_of(slot * SPT, SPT), SPT)] = block
        bt[pl.ds(pl.multiple_of(slot * SPT, SPT), SPT), :] = block.T

    def update(slot, yy):
        lanes = pl.ds(pl.multiple_of(yy * BLK, BLK), BLK)
        left = bt[pl.ds(pl.multiple_of(slot * SPT, SPT), SPT), :]
        t = jnp.dot(left, ab[:, lanes], preferred_element_type=F32).reshape(SPT // 8, 8, BLK)
        old = run[0:8, lanes]
        top = jnp.maximum(old, jnp.max(t, axis=0))
        run[8:16, lanes] = run[8:16, lanes] * jnp.exp2(old - top) + jnp.sum(jnp.exp2(t - top[None]), axis=0)
        run[0:8, lanes] = top

    def stream(slots, offsets, fresh=True):
        if fresh:
            for slot in slots:
                prep_spots(slot)
        for slot in slots:
            for dy in offsets:
                update(slot, (y + dy) & 3)

    def got(p):
        ring_copy(p).wait_recv()
        hand_on(p).start()

    prep_cells(y, 0)
    prep_cells(y, 1)
    stream([s], (0,))
    pair0.wait_recv()
    stream([z * 2 + 1 - c], (0,))
    below, above = (y + 3) & 3, (y + 1) & 3
    near[1, 0].wait_recv()
    ref = cg.at[below, 0]
    far0 = start(ref, ref, s_half.at[0], r_half.at[0], (0, 1, 0, 0))
    near[3, 1].wait_recv()
    ref = cg.at[above, 1]
    far1 = start(ref, ref, s_half.at[1], r_half.at[1], (0, 3, 0, 0))
    got(1)
    got(2)
    stream([slot_of(1, False), slot_of(2, False)], (0,))
    prep_cells(below, 0)
    prep_cells(above, 1)
    near[1, 1].wait_recv()
    prep_cells(below, 1)
    near[3, 0].wait_recv()
    prep_cells(above, 0)

    stream([s, z * 2 + 1 - c, slot_of(1, False), slot_of(2, False)], (1, 3), False)

    def four(k, carry):
        got(2 * k + 1)
        got(2 * k + 2)
        hand_on(2 * k - 1).wait_recv()
        hand_on(2 * k).wait_recv()
        stream(
            [slot_of(2 * k - 1, True), slot_of(2 * k, True), slot_of(2 * k + 1, False), slot_of(2 * k + 2, False)],
            (0, 1, 3),
        )
        return carry

    lax.fori_loop(1, 3, four, 0)
    arrive([far0, far1])
    yy = (y + 2) & 3
    prep_cells(yy, 0)
    prep_cells(yy, 1)
    stream([s, z * 2 + 1 - c] + [slot_of(p, False) for p in (1, 2, 3, 4)], (2,), False)
    got(7)
    stream([slot_of(p, True) for p in (1, 2, 3, 4)] + [slot_of(p, False) for p in (5, 6)], (2,), False)
    hand_on(5).wait_recv()
    hand_on(6).wait_recv()
    stream([slot_of(7, False), slot_of(5, True), slot_of(6, True)], (0, 1, 3, 2))
    hand_on(7).wait_recv()
    stream([slot_of(7, True)], (0, 1, 3, 2))
    top = jnp.max(run[0:8, :], axis=0, keepdims=True)
    total = jnp.sum(run[8:16, :] * jnp.exp2(run[0:8, :] - top), axis=0, keepdims=True)
    rb1[xy] = top + jnp.log2(total) - pot[0:1, :]

    def row_exchange(buf, ssem, rsem):
        return [start(buf.at[xy], buf.at[xy], ssem.at[k], rsem.at[k], peer) for k, peer in enumerate(row_peers)]

    before = len(sends)
    moving = row_exchange(rb1, s_row1, r_row1)
    for k in range(TILE // 256):
        at[k * 256 : (k + 1) * 256, :] = ab[:, k * 256 : (k + 1) * 256].T
    for h in (0, 1):
        for r in range(TILE // 256):
            rows = slice(r * 256, (r + 1) * 256)
            e[h, rows, :] = jnp.dot(at[rows, :], bb[:, h * HALF : (h + 1) * HALF], preferred_element_type=F32)
    def drain(p, carry):
        ring_copy(p).wait_send()
        hand_on(p).wait_send()
        return carry

    settled(before)
    lax.fori_loop(1, 8, drain, 0)
    arrive(lab_in)
    for k in range(4):
        pot[1:2, k * BLK : (k + 1) * BLK] = lab[k] * LOG2E
    arrive(moving)
    cell1 = pot[1:2, :] - lse(rb1[...], 0)[0]
    pot[2:3, :] = cell1
    f1, f2, f3 = pieces3(cell1 - pot[0:1, :])
    urow[0:1, :] = f1
    urow[1:2, :] = f2
    urow[2:3, :] = f3
    urow[3:8, :] = jnp.zeros((5, TILE), F32)
    sub = lax.broadcasted_iota(jnp.int32, (8, 128), 0)
    ones = jnp.where(sub < 3, 1.0, 0.0).astype(BF16)

    def to_column():
        return lax.dot_general(
            urow[...].astype(BF16), ones, (((0,), (0,)), ((), ())), preferred_element_type=F32
        )

    ucol[...] = to_column()

    def half_lanes(h):
        return pl.ds(pl.multiple_of(h * HALF, HALF), HALF)

    def col_pass(h):
        def step(r, carry):
            for q in range(2):
                at_r = r * 2 + q
                rows = pl.ds(pl.multiple_of(at_r * RB, RB), RB)
                f = ucol[rows, :]
                for k in range(HALF // 128):
                    lanes = slice(k * 128, (k + 1) * 128)
                    v = (e[h, rows, lanes] + f).reshape(RB // 8, 8, 128)
                    top = jnp.max(v, axis=0)
                    w = jnp.exp2(v - top[None])
                    e[h, rows, lanes] = w.reshape(RB, 128)
                    tops[h, at_r, :, lanes] = top
                    sums[at_r, :, lanes] = jnp.sum(w, axis=0)
            return carry

        lax.fori_loop(0, TILE // 256, step, 0)
        part = tops[h].reshape(TILE // RB * 8, HALF)
        top = jnp.max(part, axis=0, keepdims=True)
        total = jnp.sum(sums[...].reshape(TILE // RB * 8, HALF) * jnp.exp2(part - top), axis=0, keepdims=True)
        return top + jnp.log2(total)

    def ring_exchange(buf, ssem, rsem):
        return [start(buf.at[z], buf.at[z], ssem.at[k], rsem.at[k], peer) for k, peer in enumerate(ring_peers)]

    cs1[...] = col_pass(1 - c)
    half = start(cs1, cr1, s_pair.at[0], r_pair.at[0], sibling)
    mine = col_pass(c)
    half.wait_recv()
    cz1[z] = lse(jnp.concatenate([mine, cr1[...]], axis=0), 0)
    before = len(sends)
    moving = ring_exchange(cz1, s_col1, r_col1)
    settled(before)
    arrive(moving)
    gh1[c] = lbb[:, half_lanes(c)] * LOG2E - lse(cz1[...], 0)[0]
    back = start(gh1.at[c], gh1.at[c], s_pair.at[1], r_pair.at[1], sibling)

    def scales(h):
        qrow[h] = jnp.exp2(tops[h] + gh1[h])

    def row_sums(h, last):
        def step(r, carry):
            q = [qrow[h, r, :, j * 128 : (j + 1) * 128] for j in range(HALF // 128)]
            block = pl.ds(pl.multiple_of(r * RB, RB), RB)
            before = ucol[block, :] if last else None
            out = []
            for g in range(RB // 8):
                rows = pl.ds(pl.multiple_of(r * RB + g * 8, 8), 8)
                t = [e[h, rows, j * 128 : (j + 1) * 128] * q[j] for j in range(HALF // 128)]
                while len(t) > 1:
                    t = [t[j] + t[j + 1] for j in range(0, len(t), 2)]
                out.append(t[0])
            out = jnp.concatenate(out, axis=0)
            ucol[block, :] = before + out if last else out
            return carry

        lax.fori_loop(0, TILE // RB, step, 0)

    def to_row():
        for k in range(TILE // 128):
            rows = slice(k * 128, (k + 1) * 128)
            rb2[xy, :, rows] = jnp.sum(ucol[rows, :].T, axis=0, keepdims=True)

    scales(c)
    row_sums(c, False)
    back.wait_recv()
    scales(1 - c)
    row_sums(1 - c, True)
    to_row()
    before = len(sends)
    moving = row_exchange(rb2, s_row2, r_row2)
    settled(before)
    arrive(moving)
    ratio = jnp.exp2(pot[1:2, :]) / jnp.sum(rb2[...], axis=0)
    u1, u2, u3 = pieces3(ratio)
    urow[0:1, :] = u1
    urow[1:2, :] = u2
    urow[2:3, :] = u3
    ucol[...] = to_column()

    def col_sums(h):
        def step(r, t):
            out = [jnp.zeros((8, 128), F32) for k in t]
            for g in range(RB // 8):
                rows = pl.ds(pl.multiple_of(r * RB + g * 8, 8), 8)
                scale = ucol[rows, :]
                for k in range(HALF // 128):
                    out[k] = out[k] + e[h, rows, k * 128 : (k + 1) * 128] * scale
            return tuple(t[k] + out[k] * qrow[h, r, :, k * 128 : (k + 1) * 128] for k in range(HALF // 128))

        parts = lax.fori_loop(0, TILE // RB, step, tuple(jnp.zeros((8, 128), F32) for k in range(HALF // 128)))
        return jnp.sum(jnp.concatenate(parts, axis=1), axis=0, keepdims=True)

    cs2[...] = col_sums(1 - c)
    half = start(cs2, cr2, s_pair.at[2], r_pair.at[2], sibling)
    mine = col_sums(c)
    half.wait_recv()
    cz2[z] = mine + cr2[...]
    before = len(sends)
    moving = ring_exchange(cz2, s_col2, r_col2)
    fo[...] = (pot[2:3, :] + jnp.log2(ratio)) * UNSCALE
    out_f = pltpu.make_async_copy(fo.at[:, pl.ds(pl.multiple_of(y * BLK, BLK), BLK)], outf_ref, l_out.at[0])
    out_f.start()

    def halve(r, carry):
        rows = pl.ds(pl.multiple_of(r * RB, RB), RB)
        for h in (0, 1):
            for j in range(HALF // 256):
                lanes = slice(j * 256, (j + 1) * 256)
                w = (e[h, rows, lanes].reshape(RB // 8, 8, 256) * qrow[h, r, :, lanes][None]).reshape(RB, 256)
                hi = w.astype(BF16)
                eh[h, rows, lanes] = hi
                el[h, rows, lanes] = (w - hi.astype(F32)).astype(BF16)
        return carry

    lax.fori_loop(0, TILE // RB, halve, 0)
    settled(before)
    arrive(moving)
    gh2[c] = jnp.exp2(lbb[:, half_lanes(c)] * LOG2E) / jnp.sum(cz2[...], axis=0)
    back = start(gh2.at[c], gh2.at[c], s_pair.at[3], r_pair.at[3], sibling)

    def weigh(h):
        for k in range(8):
            lanes = slice(k * SPT, (k + 1) * SPT)
            v = jnp.where(row == PC, 1.0, pad_rows(sg[h * 8 + k], ROWS)) * gh2[h, :, lanes]
            hi = v.astype(BF16)
            lo = (v - hi.astype(F32)).astype(BF16)
            ptb[h, lanes, :] = jnp.concatenate([pad_rows(hi, SEC), pad_rows(lo, SEC)], axis=0).T

    def product(dy, h):
        rows = pl.ds(pl.multiple_of(((y + dy) & 3) * BLK, BLK), BLK)
        part = jnp.dot(eh[h, rows, :], ptb[h], preferred_element_type=F32)
        return part + jnp.dot(el[h, rows, :], ptb[h], preferred_element_type=F32)

    along_x, along_y, g_in = {}, [], []

    def send_x(dy, part):
        part = part.T
        part = (part[0:ROWS] + part[SEC : SEC + ROWS])[0 : PC + 1]
        for k in range(4):
            stage[dy * 4 + k] = part[:, k * SPT : (k + 1) * SPT]
        along_x[dy] = []
        for dx in (2, 1, 3):
            k = dy * 4 + dx
            src, dst = stage.at[dy * 4 + ((x + dx) & 3)], rs.at[k]
            along_x[dy].append(start(src, dst, s_rs.at[k], r_rs.at[k], (dx, 0, 0, 0)))

    def send_y(dy):
        arrive(along_x[dy])
        k = dy * 4
        xsum[dy] = (stage[k + x] + rs[k + 1]) + (rs[k + 2] + rs[k + 3])
        if dy:
            along_y.append(start(xsum.at[dy], rs.at[k], s_rs.at[k], r_rs.at[k], (0, dy, 0, 0)))

    weigh(c)
    first = product(2, c)
    back.wait_recv()
    weigh(1 - c)
    first = first + product(2, 1 - c)
    second = product(1, c) + product(1, 1 - c)
    send_x(2, first)
    for h in (0, 1):
        gbuf[y, :, h * HALF : (h + 1) * HALF] = (gh1[h] + jnp.log2(gh2[h])) * UNSCALE
    third = product(3, c) + product(3, 1 - c)
    send_x(1, second)
    send_x(3, third)
    fourth = product(0, c) + product(0, 1 - c)
    send_x(0, fourth)
    for dy in (2, 1, 3):
        send_y(dy)
    for dy in (2, 1, 3):
        g_in.append(start(gbuf.at[y], gbuf.at[y], s_g.at[dy], r_g.at[dy], (0, dy, 0, 0)))
    send_y(0)
    arrive(along_y)
    whole = (xsum[0] + rs[4]) + (rs[8] + rs[12])
    ag[x] = whole[0:PC] / whole[PC : PC + 1, :]
    mine = ag.at[x]
    before = len(sends)
    ag_in = [start(mine, mine, s_ag.at[dx], r_ag.at[dx], (dx, 0, 0, 0)) for dx in (2, 1, 3)]
    arrive(g_in)
    outs = [
        pltpu.make_async_copy(gbuf.at[k], outg_ref.at[:, pl.ds(k * TILE, TILE)], l_out.at[1 + k]) for k in range(4)
    ]
    for one in outs:
        one.start()

    def put(k, q):
        lanes = pl.ds(pl.multiple_of(k * SPT, SPT), SPT)
        outs.append(pltpu.make_async_copy(ag.at[k], outb_ref.at[:, lanes], l_out.at[5 + q]))
        outs[-1].start()

    put(x, 0)
    settled(before)
    for dx, one in reversed(list(zip((2, 1, 3), ag_in))):
        one.wait_recv()
        put((x - dx) & 3, dx)
    settled(len(sends))
    for one in [out_f] + outs:
        one.wait()


def settle(f_ref, g_ref, b_ref, outf_ref, outg_ref, outb_ref):
    outf_ref[...] = f_ref[...]
    outg_ref[...] = g_ref[...]
    outb_ref[...] = b_ref[...]


def on_device(cells_pca, spots_pca, log_a, log_b):
    dma = pltpu.SemaphoreType.DMA
    hbm = pl.BlockSpec(memory_space=pl.ANY)
    vmem = pl.BlockSpec(memory_space=pltpu.VMEM)
    shapes = (
        jax.ShapeDtypeStruct((1, BLK), F32),
        jax.ShapeDtypeStruct((1, 4 * TILE), F32),
        jax.ShapeDtypeStruct((PC, BLK), F32),
    )
    pairs = ((4, 2), (2,), (4,), (8,), (8,), (15,), (15,), (4,), (7,), (7,), (4,), (16,), (4,))
    out = pl.pallas_call(
        kernel,
        out_shape=shapes,
        in_specs=[hbm] * 4,
        out_specs=(hbm,) * 3,
        scratch_shapes=[
            pltpu.VMEM((4, 2, PC, 256), F32),
            pltpu.VMEM((4, 1, BLK), F32),
            pltpu.VMEM((1, TILE), F32),
            pltpu.VMEM((16, PC, SPT), F32),
            pltpu.VMEM((4 * SEC, TILE), BF16),
            pltpu.VMEM((4 * SEC, TILE), BF16),
            pltpu.VMEM((TILE, 4 * SEC), BF16),
            pltpu.VMEM((2, TILE, HALF), F32),
            pltpu.VMEM((16, TILE), F32),
            pltpu.VMEM((TILE, 128), F32),
            pltpu.VMEM((8, TILE), F32),
            pltpu.VMEM((16, 1, TILE), F32),
            pltpu.VMEM((16, 1, TILE), F32),
            pltpu.VMEM((1, HALF), F32),
            pltpu.VMEM((1, HALF), F32),
            pltpu.VMEM((8, 1, HALF), F32),
            pltpu.VMEM((2, 1, HALF), F32),
            pltpu.VMEM((1, HALF), F32),
            pltpu.VMEM((1, HALF), F32),
            pltpu.VMEM((8, 1, HALF), F32),
            pltpu.VMEM((2, 1, HALF), F32),
            pltpu.VMEM((4, 1, TILE), F32),
            pltpu.VMEM((16, PC + 1, SPT), F32),
            pltpu.VMEM((16, PC + 1, SPT), F32),
            pltpu.VMEM((4, PC, SPT), F32),
            pltpu.VMEM((8, TILE), F32),
            pltpu.VMEM((1, TILE), F32),
            pltpu.VMEM((2, TILE // RB, 8, HALF), F32),
            pltpu.VMEM((TILE // RB, 8, HALF), F32),
            pltpu.VMEM((2, TILE // RB, 8, HALF), F32),
            pltpu.VMEM((2, HALF, 2 * SEC), BF16),
            pltpu.VMEM((2, TILE, HALF), BF16),
            pltpu.VMEM((2, TILE, HALF), BF16),
            pltpu.VMEM((TILE, 4 * SEC), BF16),
            pltpu.VMEM((4, PC + 1, SPT), F32),
            dma((5,)),
        ]
        + [dma(n) for n in pairs for _ in range(2)]
        + [dma((9,))],
        compiler_params=pltpu.CompilerParams(
            collective_id=0, has_side_effects=True, vmem_limit_bytes=58 * 2**20
        ),
        cost_estimate=pl.CostEstimate(flops=10 * 2**30, bytes_accessed=2**20, transcendentals=2**23),
        name="sinkhorn",
    )(cells_pca, spots_pca, log_a.reshape(1, BLK), log_b.reshape(1, 4 * TILE))
    f, g, bary = pl.pallas_call(
        settle,
        out_shape=shapes,
        in_specs=[vmem] * 3,
        out_specs=(vmem,) * 3,
        name="settle",
    )(*out)
    return f.reshape(BLK), g.reshape(4 * TILE), bary


def solution(mesh):
    placed = (P(None, "cell"), P(None, ("spot", "cell")), P("cell"), P("spot"))
    return jax.shard_map(
        on_device,
        mesh=mesh,
        in_specs=placed,
        out_specs=(P("cell"), P("spot"), P(None, "cell")),
        check_vma=False,
    )
```

```python
import math

import jax
import jax.numpy as jnp
from jax import lax
from jax.experimental import pallas as pl
from jax.experimental.pallas import tpu as pltpu
from jax.sharding import PartitionSpec as P

MESH = pl.DeviceIdType.MESH
F32, BF16 = jnp.float32, jnp.bfloat16

PC = 50
ROWS = 56
SEC = 64
TILE = 2048
BLK = 512
HALF = TILE // 2
SPT = 128
RB = 128
blur = 0.25
LOG2E = math.log2(math.e)
SCALE = LOG2E / blur
UNSCALE = blur / LOG2E


def pieces3(v):
    one = v.astype(BF16).astype(F32)
    rest = v - one
    two = rest.astype(BF16).astype(F32)
    return one, two, (rest - two).astype(BF16).astype(F32)


def pad_rows(v, rows):
    return jnp.concatenate([v, jnp.zeros((rows - v.shape[0], v.shape[1]), v.dtype)], axis=0)


def lse(v, axis):
    top = jnp.max(v, axis=axis, keepdims=True)
    out = top + jnp.log2(jnp.sum(jnp.exp2(v - top), axis=axis, keepdims=True))
    return out


def kernel(
    cells_ref, spots_ref, loga_ref, logb_ref, outf_ref, outg_ref, outb_ref,
    cg, lab, lbb, sg, ab, bb, at, e, run, ucol, urow, rb1, rb2, cs1, cr1, cz1, gh1, cs2, cr2, cz2, gh2, gbuf, stage, rs, ag,
    pot, fo, tops, sums, qrow, ptb, eh, el, bt, xsum,
    l_in, s_cell, r_cell, s_half, r_half, s_lab, r_lab, s_spot, r_spot, s_core, r_core, s_row1, r_row1, s_row2, r_row2,
    s_pair, r_pair, s_col1, r_col1, s_col2, r_col2, s_g, r_g, s_rs, r_rs, s_ag, r_ag, l_out,
):
    b = lax.axis_index("cell")
    x = lax.axis_index("spot")
    s = b & 15
    y, z, c = b // 16, s // 2, b & 1
    xy = x * 4 + y

    def dev(dx, dy, dz, dc):
        px, py, pz, pc = (x + dx) & 3, (y + dy) & 3, (z + dz) & 7, (c + dc) & 1
        return ((py * 8 + pz) * 2 + pc, px)

    row_peers = [(dx, dy, 0, 0) for dx in (2, 1, 3, 0) for dy in (2, 1, 3, 0) if dx or dy]
    ring = (4, 3, 5, 2, 6, 1, 7)
    ring_peers = [(0, 0, dz, 0) for dz in ring]
    sibling = (0, 0, 0, 1)
    peers = row_peers + ring_peers + [sibling]
    barrier = pltpu.get_barrier_semaphore()
    for peer in peers:
        pl.semaphore_signal(barrier, inc=1, device_id=dev(*peer), device_id_type=MESH)

    loads = [
        pltpu.make_async_copy(cells_ref.at[:, pl.ds(0, 256)], cg.at[y, 0], l_in.at[0]),
        pltpu.make_async_copy(cells_ref.at[:, pl.ds(256, 256)], cg.at[y, 1], l_in.at[1]),
        pltpu.make_async_copy(spots_ref, sg.at[s], l_in.at[2]),
        pltpu.make_async_copy(loga_ref, lab.at[y], l_in.at[3]),
        pltpu.make_async_copy(logb_ref.at[:, pl.ds(pl.multiple_of(y * TILE, TILE), TILE)], lbb, l_in.at[4]),
    ]
    for one in loads:
        one.start()
    run[0:8, :] = jnp.full((8, TILE), -jnp.inf, F32)
    run[8:16, :] = jnp.zeros((8, TILE), F32)
    for one in loads:
        one.wait()
    pl.semaphore_wait(barrier, len(peers))

    sends = []

    def copy(src, dst, ssem, rsem, peer):
        return pltpu.make_async_remote_copy(
            src_ref=src, dst_ref=dst, send_sem=ssem, recv_sem=rsem, device_id=dev(*peer), device_id_type=MESH
        )

    def start(*args):
        one = copy(*args)
        one.start()
        sends.append(one)
        return one

    def arrive(copies):
        for one in copies:
            one.wait_recv()

    near = {}
    for dy, h in ((1, 0), (3, 1), (1, 1), (3, 0)):
        ref = cg.at[y, h]
        near[dy, h] = start(ref, ref, s_cell.at[dy, h], r_cell.at[dy, h], (0, dy, 0, 0))

    def turn(p):
        return jnp.where((p & 1) == 1, (p + 1) // 2, 8 - p // 2)

    def slot_of(p, other):
        return ((z + 8 - turn(p)) & 7) * 2 + (1 - c if other else c)

    def ring_copy(p):
        ref = sg.at[s]
        return copy(ref, ref, s_spot.at[p], r_spot.at[p], (0, 0, turn(p), 0))

    def hand_on(p):
        ref = sg.at[slot_of(p, False)]
        return copy(ref, ref, s_core.at[p], r_core.at[p], sibling)

    own = sg.at[s]
    pair0 = start(own, own, s_core.at[0], r_core.at[0], sibling)
    lax.fori_loop(1, 8, lambda p, carry: (ring_copy(p).start(), carry)[1], 0)
    lab_in = [start(lab.at[y], lab.at[y], s_lab.at[dy], r_lab.at[dy], (0, dy, 0, 0)) for dy in (1, 2, 3)]

    row = lax.broadcasted_iota(jnp.int32, (ROWS, 1), 0)
    centre = jnp.sum(sg[s], axis=1, keepdims=True) * (1.0 / SPT)

    def stack(v, extra, order):
        hi = v.astype(BF16)
        lo = (v - hi.astype(F32)).astype(BF16)
        first = pad_rows((hi.astype(F32) + extra).astype(BF16), SEC)
        hi, lo = pad_rows(hi, SEC), pad_rows(lo, SEC)
        return jnp.concatenate([first] + [(hi, lo)[k] for k in order], axis=0)

    def prep_cells(yy, h):
        lanes = pl.ds(pl.multiple_of(yy * BLK + h * 256, 256), 256)
        v = pad_rows(cg[yy, h] - centre, ROWS)
        pot[0:1, lanes] = jnp.sum(v * v, axis=0, keepdims=True) * SCALE
        extra = jnp.where((row >= PC) & (row < PC + 3), 1.0, 0.0) + jnp.zeros((ROWS, 256), F32)
        ab[:, lanes] = stack(v * (2.0 * SCALE), extra, (0, 1, 1))

    def prep_spots(slot):
        v = pad_rows(sg[slot] - centre, ROWS)
        norm = jnp.sum(v * v, axis=0, keepdims=True) * (-SCALE)
        n1, n2, n3 = pieces3(norm)
        extra = jnp.where(row == PC, n1, 0.0) + jnp.where(row == PC + 1, n2, 0.0) + jnp.where(row == PC + 2, n3, 0.0)
        extra = extra + jnp.where((row >= PC + 3) & (row < PC + 6), 1.0, 0.0)
        block = stack(v, extra, (1, 0, 1))
        bb[:, pl.ds(pl.multiple_of(slot * SPT, SPT), SPT)] = block
        bt[pl.ds(pl.multiple_of(slot * SPT, SPT), SPT), :] = block.T

    def update(slot, yy):
        lanes = pl.ds(pl.multiple_of(yy * BLK, BLK), BLK)
        left = bt[pl.ds(pl.multiple_of(slot * SPT, SPT), SPT), :]
        t = jnp.dot(left, ab[:, lanes], preferred_element_type=F32).reshape(SPT // 8, 8, BLK)
        old = run[0:8, lanes]
        top = jnp.maximum(old, jnp.max(t, axis=0))
        run[8:16, lanes] = run[8:16, lanes] * jnp.exp2(old - top) + jnp.sum(jnp.exp2(t - top[None]), axis=0)
        run[0:8, lanes] = top

    def stream(slots, offsets, fresh=True):
        if fresh:
            for slot in slots:
                prep_spots(slot)
        for slot in slots:
            for dy in offsets:
                update(slot, (y + dy) & 3)

    def got(p):
        ring_copy(p).wait_recv()
        hand_on(p).start()

    prep_cells(y, 0)
    prep_cells(y, 1)
    stream([s], (0,))
    below, above = (y + 3) & 3, (y + 1) & 3
    near[1, 0].wait_recv()
    ref = cg.at[below, 0]
    far0 = start(ref, ref, s_half.at[0], r_half.at[0], (0, 1, 0, 0))
    near[3, 1].wait_recv()
    ref = cg.at[above, 1]
    far1 = start(ref, ref, s_half.at[1], r_half.at[1], (0, 3, 0, 0))
    pair0.wait_recv()
    got(1)
    got(2)
    stream([z * 2 + 1 - c, slot_of(1, False), slot_of(2, False)], (0,))
    prep_cells(below, 0)
    prep_cells(above, 1)
    near[1, 1].wait_recv()
    prep_cells(below, 1)
    near[3, 0].wait_recv()
    prep_cells(above, 0)

    stream([s, z * 2 + 1 - c, slot_of(1, False), slot_of(2, False)], (1, 3), False)

    def four(k, carry):
        got(2 * k + 1)
        got(2 * k + 2)
        hand_on(2 * k - 1).wait_recv()
        hand_on(2 * k).wait_recv()
        stream(
            [slot_of(2 * k - 1, True), slot_of(2 * k, True), slot_of(2 * k + 1, False), slot_of(2 * k + 2, False)],
            (0, 1, 3),
        )
        return carry

    lax.fori_loop(1, 3, four, 0)
    arrive([far0, far1])
    yy = (y + 2) & 3
    prep_cells(yy, 0)
    prep_cells(yy, 1)
    stream([s, z * 2 + 1 - c] + [slot_of(p, False) for p in (1, 2, 3, 4)], (2,), False)
    got(7)
    stream([slot_of(p, True) for p in (1, 2, 3, 4)] + [slot_of(p, False) for p in (5, 6)], (2,), False)
    hand_on(5).wait_recv()
    hand_on(6).wait_recv()
    stream([slot_of(7, False), slot_of(5, True), slot_of(6, True)], (0, 1, 3, 2))
    hand_on(7).wait_recv()
    stream([slot_of(7, True)], (0, 1, 3, 2))
    top = jnp.max(run[0:8, :], axis=0, keepdims=True)
    total = jnp.sum(run[8:16, :] * jnp.exp2(run[0:8, :] - top), axis=0, keepdims=True)
    rb1[xy] = top + jnp.log2(total) - pot[0:1, :]

    def row_exchange(buf, ssem, rsem):
        return [start(buf.at[xy], buf.at[xy], ssem.at[k], rsem.at[k], peer) for k, peer in enumerate(row_peers)]

    moving = row_exchange(rb1, s_row1, r_row1)
    for k in range(TILE // 256):
        at[k * 256 : (k + 1) * 256, :] = ab[:, k * 256 : (k + 1) * 256].T
    for h in (0, 1):
        for r in range(TILE // 256):
            rows = slice(r * 256, (r + 1) * 256)
            e[h, rows, :] = jnp.dot(at[rows, :], bb[:, h * HALF : (h + 1) * HALF], preferred_element_type=F32)
    arrive(lab_in)
    for k in range(4):
        pot[1:2, k * BLK : (k + 1) * BLK] = lab[k] * LOG2E
    arrive(moving)
    cell1 = pot[1:2, :] - lse(rb1[...], 0)[0]
    pot[2:3, :] = cell1
    f1, f2, f3 = pieces3(cell1 - pot[0:1, :])
    urow[0:1, :] = f1
    urow[1:2, :] = f2
    urow[2:3, :] = f3
    urow[3:8, :] = jnp.zeros((5, TILE), F32)
    sub = lax.broadcasted_iota(jnp.int32, (8, 128), 0)
    ones = jnp.where(sub < 3, 1.0, 0.0).astype(BF16)

    def to_column():
        return lax.dot_general(
            urow[...].astype(BF16), ones, (((0,), (0,)), ((), ())), preferred_element_type=F32
        )

    ucol[...] = to_column()

    def half_lanes(h):
        return pl.ds(pl.multiple_of(h * HALF, HALF), HALF)

    def col_pass(h):
        def step(r, carry):
            for q in range(2):
                at_r = r * 2 + q
                rows = pl.ds(pl.multiple_of(at_r * RB, RB), RB)
                f = ucol[rows, :]
                for k in range(HALF // 128):
                    lanes = slice(k * 128, (k + 1) * 128)
                    v = (e[h, rows, lanes] + f).reshape(RB // 8, 8, 128)
                    top = jnp.max(v, axis=0)
                    w = jnp.exp2(v - top[None])
                    e[h, rows, lanes] = w.reshape(RB, 128)
                    tops[h, at_r, :, lanes] = top
                    sums[at_r, :, lanes] = jnp.sum(w, axis=0)
            return carry

        lax.fori_loop(0, TILE // 256, step, 0)
        part = tops[h].reshape(TILE // RB * 8, HALF)
        top = jnp.max(part, axis=0, keepdims=True)
        total = jnp.sum(sums[...].reshape(TILE // RB * 8, HALF) * jnp.exp2(part - top), axis=0, keepdims=True)
        return top + jnp.log2(total)

    def ring_exchange(buf, ssem, rsem):
        return [start(buf.at[z], buf.at[z], ssem.at[k], rsem.at[k], peer) for k, peer in enumerate(ring_peers)]

    cs1[...] = col_pass(1 - c)
    half = start(cs1, cr1, s_pair.at[0], r_pair.at[0], sibling)
    mine = col_pass(c)
    half.wait_recv()
    cz1[z] = lse(jnp.concatenate([mine, cr1[...]], axis=0), 0)
    arrive(ring_exchange(cz1, s_col1, r_col1))
    gh1[c] = lbb[:, half_lanes(c)] * LOG2E - lse(cz1[...], 0)[0]
    back = start(gh1.at[c], gh1.at[c], s_pair.at[1], r_pair.at[1], sibling)

    def scales(h):
        qrow[h] = jnp.exp2(tops[h] + gh1[h])

    def row_sums(h, last):
        def step(r, carry):
            q = [qrow[h, r, :, j * 128 : (j + 1) * 128] for j in range(HALF // 128)]
            block = pl.ds(pl.multiple_of(r * RB, RB), RB)
            before = ucol[block, :] if last else None
            out = []
            for g in range(RB // 8):
                rows = pl.ds(pl.multiple_of(r * RB + g * 8, 8), 8)
                t = [e[h, rows, j * 128 : (j + 1) * 128] * q[j] for j in range(HALF // 128)]
                while len(t) > 1:
                    t = [t[j] + t[j + 1] for j in range(0, len(t), 2)]
                out.append(t[0])
            out = jnp.concatenate(out, axis=0)
            ucol[block, :] = before + out if last else out
            return carry

        lax.fori_loop(0, TILE // RB, step, 0)

    def to_row():
        for k in range(TILE // 128):
            rows = slice(k * 128, (k + 1) * 128)
            rb2[xy, :, rows] = jnp.sum(ucol[rows, :].T, axis=0, keepdims=True)

    scales(c)
    row_sums(c, False)
    back.wait_recv()
    scales(1 - c)
    row_sums(1 - c, True)
    to_row()
    arrive(row_exchange(rb2, s_row2, r_row2))
    ratio = jnp.exp2(pot[1:2, :]) / jnp.sum(rb2[...], axis=0)
    u1, u2, u3 = pieces3(ratio)
    urow[0:1, :] = u1
    urow[1:2, :] = u2
    urow[2:3, :] = u3
    ucol[...] = to_column()

    def col_sums(h):
        def step(r, t):
            out = [jnp.zeros((8, 128), F32) for k in t]
            for g in range(RB // 8):
                rows = pl.ds(pl.multiple_of(r * RB + g * 8, 8), 8)
                scale = ucol[rows, :]
                for k in range(HALF // 128):
                    out[k] = out[k] + e[h, rows, k * 128 : (k + 1) * 128] * scale
            return tuple(t[k] + out[k] * qrow[h, r, :, k * 128 : (k + 1) * 128] for k in range(HALF // 128))

        parts = lax.fori_loop(0, TILE // RB, step, tuple(jnp.zeros((8, 128), F32) for k in range(HALF // 128)))
        return jnp.sum(jnp.concatenate(parts, axis=1), axis=0, keepdims=True)

    cs2[...] = col_sums(1 - c)
    half = start(cs2, cr2, s_pair.at[2], r_pair.at[2], sibling)
    mine = col_sums(c)
    half.wait_recv()
    cz2[z] = mine + cr2[...]
    moving = ring_exchange(cz2, s_col2, r_col2)
    fo[...] = (pot[2:3, :] + jnp.log2(ratio)) * UNSCALE
    out_f = pltpu.make_async_copy(fo.at[:, pl.ds(pl.multiple_of(y * BLK, BLK), BLK)], outf_ref, l_out.at[0])
    out_f.start()

    def halve(r, carry):
        rows = pl.ds(pl.multiple_of(r * RB, RB), RB)
        for h in (0, 1):
            for j in range(HALF // 256):
                lanes = slice(j * 256, (j + 1) * 256)
                w = (e[h, rows, lanes].reshape(RB // 8, 8, 256) * qrow[h, r, :, lanes][None]).reshape(RB, 256)
                hi = w.astype(BF16)
                eh[h, rows, lanes] = hi
                el[h, rows, lanes] = (w - hi.astype(F32)).astype(BF16)
        return carry

    lax.fori_loop(0, TILE // RB, halve, 0)
    arrive(moving)
    gh2[c] = jnp.exp2(lbb[:, half_lanes(c)] * LOG2E) / jnp.sum(cz2[...], axis=0)
    back = start(gh2.at[c], gh2.at[c], s_pair.at[3], r_pair.at[3], sibling)

    def weigh(h):
        for k in range(8):
            lanes = slice(k * SPT, (k + 1) * SPT)
            v = jnp.where(row == PC, 1.0, pad_rows(sg[h * 8 + k], ROWS)) * gh2[h, :, lanes]
            hi = v.astype(BF16)
            lo = (v - hi.astype(F32)).astype(BF16)
            ptb[h, lanes, :] = jnp.concatenate([pad_rows(hi, SEC), pad_rows(lo, SEC)], axis=0).T

    def product(dy, h):
        rows = pl.ds(pl.multiple_of(((y + dy) & 3) * BLK, BLK), BLK)
        part = jnp.dot(eh[h, rows, :], ptb[h], preferred_element_type=F32)
        return part + jnp.dot(el[h, rows, :], ptb[h], preferred_element_type=F32)

    along_x, along_y, g_in = {}, [], []

    def send_x(dy, part):
        part = part.T
        part = (part[0:ROWS] + part[SEC : SEC + ROWS])[0 : PC + 1]
        for k in range(4):
            stage[dy * 4 + k] = part[:, k * SPT : (k + 1) * SPT]
        along_x[dy] = []
        for dx in (2, 1, 3):
            k = dy * 4 + dx
            src, dst = stage.at[dy * 4 + ((x + dx) & 3)], rs.at[k]
            along_x[dy].append(start(src, dst, s_rs.at[k], r_rs.at[k], (dx, 0, 0, 0)))

    def send_y(dy):
        arrive(along_x[dy])
        k = dy * 4
        xsum[dy] = (stage[k + x] + rs[k + 1]) + (rs[k + 2] + rs[k + 3])
        if dy:
            along_y.append(start(xsum.at[dy], rs.at[k], s_rs.at[k], r_rs.at[k], (0, dy, 0, 0)))

    weigh(c)
    first = product(2, c)
    back.wait_recv()
    weigh(1 - c)
    first = first + product(2, 1 - c)
    second = product(1, c) + product(1, 1 - c)
    send_x(2, first)
    for h in (0, 1):
        gbuf[y, :, h * HALF : (h + 1) * HALF] = (gh1[h] + jnp.log2(gh2[h])) * UNSCALE
    third = product(3, c) + product(3, 1 - c)
    send_x(1, second)
    send_x(3, third)
    fourth = product(0, c) + product(0, 1 - c)
    send_x(0, fourth)
    for dy in (2, 1, 3):
        send_y(dy)
    for dy in (2, 1, 3):
        g_in.append(start(gbuf.at[y], gbuf.at[y], s_g.at[dy], r_g.at[dy], (0, dy, 0, 0)))
    send_y(0)
    arrive(along_y)
    whole = (xsum[0] + rs[4]) + (rs[8] + rs[12])
    ag[x] = whole[0:PC] / whole[PC : PC + 1, :]
    mine = ag.at[x]
    ag_in = [start(mine, mine, s_ag.at[dx], r_ag.at[dx], (dx, 0, 0, 0)) for dx in (2, 1, 3)]
    arrive(g_in)
    outs = [
        pltpu.make_async_copy(gbuf.at[k], outg_ref.at[:, pl.ds(k * TILE, TILE)], l_out.at[1 + k]) for k in range(4)
    ]
    for one in outs:
        one.start()

    def put(k, q):
        lanes = pl.ds(pl.multiple_of(k * SPT, SPT), SPT)
        outs.append(pltpu.make_async_copy(ag.at[k], outb_ref.at[:, lanes], l_out.at[5 + q]))
        outs[-1].start()

    put(x, 0)
    for dx, one in reversed(list(zip((2, 1, 3), ag_in))):
        one.wait_recv()
        put((x - dx) & 3, dx)
    for one in sends:
        one.wait_send()

    def drain(p, carry):
        ring_copy(p).wait_send()
        hand_on(p).wait_send()
        return carry

    lax.fori_loop(1, 8, drain, 0)
    for one in [out_f] + outs:
        one.wait()


def settle(f_ref, g_ref, b_ref, outf_ref, outg_ref, outb_ref):
    outf_ref[...] = f_ref[...]
    outg_ref[...] = g_ref[...]
    outb_ref[...] = b_ref[...]


def on_device(cells_pca, spots_pca, log_a, log_b):
    dma = pltpu.SemaphoreType.DMA
    hbm = pl.BlockSpec(memory_space=pl.ANY)
    vmem = pl.BlockSpec(memory_space=pltpu.VMEM)
    shapes = (
        jax.ShapeDtypeStruct((1, BLK), F32),
        jax.ShapeDtypeStruct((1, 4 * TILE), F32),
        jax.ShapeDtypeStruct((PC, BLK), F32),
    )
    pairs = ((4, 2), (2,), (4,), (8,), (8,), (15,), (15,), (4,), (7,), (7,), (4,), (16,), (4,))
    out = pl.pallas_call(
        kernel,
        out_shape=shapes,
        in_specs=[hbm] * 4,
        out_specs=(hbm,) * 3,
        scratch_shapes=[
            pltpu.VMEM((4, 2, PC, 256), F32),
            pltpu.VMEM((4, 1, BLK), F32),
            pltpu.VMEM((1, TILE), F32),
            pltpu.VMEM((16, PC, SPT), F32),
            pltpu.VMEM((4 * SEC, TILE), BF16),
            pltpu.VMEM((4 * SEC, TILE), BF16),
            pltpu.VMEM((TILE, 4 * SEC), BF16),
            pltpu.VMEM((2, TILE, HALF), F32),
            pltpu.VMEM((16, TILE), F32),
            pltpu.VMEM((TILE, 128), F32),
            pltpu.VMEM((8, TILE), F32),
            pltpu.VMEM((16, 1, TILE), F32),
            pltpu.VMEM((16, 1, TILE), F32),
            pltpu.VMEM((1, HALF), F32),
            pltpu.VMEM((1, HALF), F32),
            pltpu.VMEM((8, 1, HALF), F32),
            pltpu.VMEM((2, 1, HALF), F32),
            pltpu.VMEM((1, HALF), F32),
            pltpu.VMEM((1, HALF), F32),
            pltpu.VMEM((8, 1, HALF), F32),
            pltpu.VMEM((2, 1, HALF), F32),
            pltpu.VMEM((4, 1, TILE), F32),
            pltpu.VMEM((16, PC + 1, SPT), F32),
            pltpu.VMEM((16, PC + 1, SPT), F32),
            pltpu.VMEM((4, PC, SPT), F32),
            pltpu.VMEM((8, TILE), F32),
            pltpu.VMEM((1, TILE), F32),
            pltpu.VMEM((2, TILE // RB, 8, HALF), F32),
            pltpu.VMEM((TILE // RB, 8, HALF), F32),
            pltpu.VMEM((2, TILE // RB, 8, HALF), F32),
            pltpu.VMEM((2, HALF, 2 * SEC), BF16),
            pltpu.VMEM((2, TILE, HALF), BF16),
            pltpu.VMEM((2, TILE, HALF), BF16),
            pltpu.VMEM((TILE, 4 * SEC), BF16),
            pltpu.VMEM((4, PC + 1, SPT), F32),
            dma((5,)),
        ]
        + [dma(n) for n in pairs for _ in range(2)]
        + [dma((9,))],
        compiler_params=pltpu.CompilerParams(
            collective_id=0, has_side_effects=True, vmem_limit_bytes=58 * 2**20
        ),
        cost_estimate=pl.CostEstimate(flops=10 * 2**30, bytes_accessed=2**20, transcendentals=2**23),
        name="sinkhorn",
    )(cells_pca, spots_pca, log_a.reshape(1, BLK), log_b.reshape(1, 4 * TILE))
    f, g, bary = pl.pallas_call(
        settle,
        out_shape=shapes,
        in_specs=[vmem] * 3,
        out_specs=(vmem,) * 3,
        name="settle",
    )(*out)
    return f.reshape(BLK), g.reshape(4 * TILE), bary


def solution(mesh):
    placed = (P(None, "cell"), P(None, ("spot", "cell")), P("cell"), P("spot"))
    return jax.shard_map(
        on_device,
        mesh=mesh,
        in_specs=placed,
        out_specs=(P("cell"), P("spot"), P(None, "cell")),
        check_vma=False,
    )
```
